512 devices in a mesh: patch: 64 (over z, y_lo, core), head: 8 (over y_hi, x).
Axes of the slice: x: 4, y: 8 (y_hi: 2, y_lo: 4; y = y_hi * 4 + y_lo), z: 8, core: 2. Of those that a mesh axis runs over, the one named last changes fastest.
Arguments:
- query_first: bfloat16 [4096, 3072], P(('patch', 'head')), may hold values from -256 to 256
- key_first: bfloat16 [4096, 3072], P(('patch', 'head')), may hold values from -8 to 8
- value_first: bfloat16 [4096, 3072], P(('patch', 'head')), may hold values from -6 to 6
- query_second: bfloat16 [4096, 3072], P(('patch', 'head')), may hold values from -256 to 256
- key_second: bfloat16 [4096, 3072], P(('patch', 'head')), may hold values from -6 to 6
- value_second: bfloat16 [4096, 3072], P(('patch', 'head')), may hold values from -6 to 6
- key_stale: bfloat16 [4096, 3072], P('patch', 'head'), may hold values from -8 to 8
- value_stale: bfloat16 [4096, 3072], P('patch', 'head'), may hold values from -6 to 6
- gate_table: float32 [50, 3072], P(None, 'head'), may hold values from 4 to 40
- step_index: int32 [2], replicated, may hold values from 0 to 49
Outputs:
- out_first: bfloat16 [4096, 3072], P(('patch', 'head'))
- out_second: bfloat16 [4096, 3072], P(('patch', 'head'))
The draws below stay inside these ranges and needn't reach their ends.
All inputs are finite; a program needn't handle non-finite values.
Results may differ from the reference program's by a relative error of at most 0.0054.
Values may be sent and summed in bfloat16 or wider, within the bound.
No kernel may reach another device: no remote copies, remote signals or barrier semaphores. Data moves between devices by JAX's collectives and lax.ppermute only.
A program may use at most 64 MiB of HBM per device.

```python
import math
import jax
import jax.numpy as jnp
from jax import lax

HDIM = 128
HEADS = 24
PATCH = 64
STEPS = 50
TOKENS = 4096
N_PATCH = 64


def base_keys(key):
    shape = (TOKENS, HEADS * HDIM)
    older = jnp.clip(jax.random.normal(jax.random.fold_in(key, 101), shape, jnp.float32), -6.0, 6.0)
    newer = jnp.clip(jax.random.normal(jax.random.fold_in(key, 202), shape, jnp.float32), -6.0, 6.0)
    return (older, newer)


def draw_query_first(key, part):
    key = jax.random.fold_in(key, 1)
    values = jnp.clip(jax.random.normal(key, (TOKENS, HEADS * HDIM), jnp.float32), -6.0, 6.0)
    return values.astype(jnp.bfloat16)


def draw_query_second(key, part):
    key = jax.random.fold_in(key, 2)
    values = jnp.clip(jax.random.normal(key, (TOKENS, HEADS * HDIM), jnp.float32), -6.0, 6.0)
    return values.astype(jnp.bfloat16)


def draw_key_stale(key, part):
    older, newer = base_keys(key)
    return older.astype(jnp.bfloat16)


def draw_key_first(key, part):
    older, newer = base_keys(key)
    return newer.astype(jnp.bfloat16)


def levels(own_key, extent, cuts, smallest, high):
    loudness, own = 1.0, jax.random.fold_in(own_key, 6)
    for dim, blocks in cuts:
        heights = jnp.exp(jax.random.uniform(jax.random.fold_in(own, dim), (blocks,), jnp.float32, smallest / len(cuts), high / len(cuts)))
        loudness = loudness * jnp.repeat(heights, extent[dim] // blocks).reshape([-1 if axis == dim else 1 for axis in range(len(extent))])
    return loudness


def scatter_about(stream_key, extent, deviation, most, shards=(), kind=jnp.bfloat16):
    entries = deviation * jax.random.normal(stream_key, extent, jnp.float32)
    if shards:
        entries = entries * levels(stream_key, extent, shards, -0.22, 0.18)
    return jnp.clip(entries, -most, most).astype(kind)


def setup_inputs(seed: int = 0) -> dict:
    key_of = jax.random.split(jax.random.key(seed), 11)
    return {
        "query_first": draw_query_first(jax.random.fold_in(key_of[10], 71), 0),
        "key_first": draw_key_first(jax.random.fold_in(key_of[10], 71), 0),
        "value_first": scatter_about(key_of[2], (TOKENS, HEADS * HDIM), 1.0, 6.0, ((0, 512),)),
        "query_second": draw_query_second(jax.random.fold_in(key_of[10], 71), 0),
        "key_second": scatter_about(key_of[4], (TOKENS, HEADS * HDIM), 1.0, 6.0, ((0, 512),)),
        "value_second": scatter_about(key_of[5], (TOKENS, HEADS * HDIM), 1.0, 6.0, ((0, 512),)),
        "key_stale": draw_key_stale(jax.random.fold_in(key_of[10], 71), 0),
        "value_stale": scatter_about(key_of[7], (TOKENS, HEADS * HDIM), 1.0, 6.0, ((0, 64), (1, 8))),
        "gate_table": jnp.clip(jnp.exp(math.log(40.0) - 2.3025851 * jax.random.uniform(key_of[8], (STEPS, HEADS * HDIM), jnp.float32) ** levels(key_of[8], (STEPS, HEADS * HDIM), ((1, 8),), -0.2, 0.2)), 4.0, 40.0),
        "step_index": jax.random.randint(key_of[9], (2,), 0, STEPS).astype(jnp.int32),
    }


def attend(queries, keys, values):
    rows = queries.shape[0]
    qh = queries.reshape(rows, HEADS, HDIM).astype(jnp.float32)
    kh = keys.reshape(-1, HEADS, HDIM).astype(jnp.float32)
    scores = jnp.einsum("qhd,khd->hqk", qh, kh) * (HDIM ** -0.5)
    top = jnp.max(scores, axis=2, keepdims=True)
    weights = jnp.exp(scores - top)
    total = jnp.sum(weights, axis=2)
    probs = weights.astype(jnp.bfloat16).astype(jnp.float32)
    vh = values.reshape(-1, HEADS, HDIM).astype(jnp.float32)
    mixed = jnp.einsum("hqk,khd->qhd", probs, vh)
    return mixed / jnp.transpose(total)[:, :, None]


def pick_gate(gate_table, step_index, which):
    selector = jnp.arange(STEPS, dtype=jnp.int32) == step_index[which]
    return jnp.sum(jnp.where(selector[:, None], gate_table, 0.0), axis=0)


def one_step(queries, fresh_keys, fresh_values, older_keys, older_values, gate_row):
    def one_patch(index):
        start = (index * PATCH).astype(jnp.int32)
        keys = lax.dynamic_update_slice_in_dim(older_keys, lax.dynamic_slice_in_dim(fresh_keys, start, PATCH, 0), start, 0)
        values = lax.dynamic_update_slice_in_dim(older_values, lax.dynamic_slice_in_dim(fresh_values, start, PATCH, 0), start, 0)
        block = lax.dynamic_slice_in_dim(queries, start, PATCH, 0)
        mixed = attend(block, keys, values).reshape(PATCH, HEADS * HDIM)
        return (mixed * gate_row).astype(jnp.bfloat16)

    blocks = lax.map(one_patch, jnp.arange(N_PATCH, dtype=jnp.int32))
    return blocks.reshape(TOKENS, HEADS * HDIM)


def reference(query_first, key_first, value_first, query_second, key_second, value_second, key_stale, value_stale, gate_table, step_index):
    out_first = one_step(query_first, key_first, value_first, key_stale, value_stale, pick_gate(gate_table, step_index, 0))
    out_second = one_step(query_second, key_second, value_second, key_stale, value_stale, pick_gate(gate_table, step_index, 1))
    return out_first, out_second
```

```python
import functools

import jax
import jax.numpy as jnp
from jax import lax
from jax.experimental import pallas as pl
from jax.experimental.pallas import tpu as pltpu
from jax.sharding import Mesh
from jax.sharding import PartitionSpec as P

HDIM = 128
GROUP = 3
WIDTH = GROUP * HDIM
NZ, NY, NC, NH, NX = 8, 4, 2, 2, 4
NHEAD = NH * NX
PEERS = NY * NHEAD
TOK = 8
PATCH = TOK * NHEAD
FRESH = 2 * TOK // NY
BLOCK = 2 * TOK + 2 * FRESH
SCALE2 = HDIM ** (-0.5) * 1.4426950408889634
LN2 = 0.6931471805599453
NEG = -1e30
F32 = jnp.float32
BF16 = jnp.bfloat16
PLANE = ("y", "h", "x")


def pack_kernel(q1, k1, v1, q2, k2, v2, ks, vs, out, kv):
    kv[:, 0:WIDTH] = ks[...]
    kv[:, WIDTH : 2 * WIDTH] = vs[...]
    share = TOK // NY
    for g in range(NHEAD):
        cols = slice(g * WIDTH, (g + 1) * WIDTH)
        queries = jnp.concatenate([q1[:, cols].astype(F32), q2[:, cols].astype(F32)], axis=0).astype(BF16)
        fresh = [ref[:, cols].astype(F32) for ref in (k1, k2, v1, v2)]
        for y in range(NY):
            rows = slice(y * share, (y + 1) * share)
            part = jnp.concatenate([f[rows] for f in fresh], axis=0).astype(BF16)
            out[y * NHEAD + g, 0 : 2 * TOK, :] = queries
            out[y * NHEAD + g, 2 * TOK : BLOCK, :] = part


def split3(x):
    hi = x.astype(BF16)
    rest = x - hi.astype(F32)
    mid = rest.astype(BF16)
    lo = (rest - mid.astype(F32)).astype(BF16)
    return hi, mid, lo


def nt_dot(a, b):
    return lax.dot_general(a, b, (((1,), (1,)), ((), ())), preferred_element_type=F32)


def attend_kernel(where_ref, step_ref, recv, own, other, gates, out):
    my_z = where_ref[0]
    my_y = where_ref[1]
    keys = NZ * PATCH
    rows = 2 * PATCH
    fresh_rows = NHEAD * 2 * FRESH
    col = lax.broadcasted_iota(jnp.int32, (1, keys), 1)
    own_bias = jnp.where(col // PATCH == my_z, NEG, 0.0)
    q_step = (lax.broadcasted_iota(jnp.int32, (rows, fresh_rows), 0) // TOK) % 2
    f_kind = lax.broadcasted_iota(jnp.int32, (rows, fresh_rows), 1) % (2 * FRESH) // (FRESH // 2)
    fresh_bias = jnp.where(f_kind == q_step, 0.0, NEG)
    at = lax.broadcasted_iota(jnp.int32, (fresh_rows, fresh_rows), 0)
    to = lax.broadcasted_iota(jnp.int32, (fresh_rows, fresh_rows), 1)
    shift = jnp.where(to == at + FRESH, 1.0, 0.0).astype(BF16)
    gate0 = gates[pl.ds(step_ref[0], 1), :]
    gate1 = gates[pl.ds(step_ref[1], 1), :]
    lane = lax.broadcasted_iota(jnp.int32, (rows, HDIM), 1)
    step_of_row = (lax.broadcasted_iota(jnp.int32, (rows, HDIM), 0) // TOK) % 2
    for y in range(NY):
        blocks = slice(y * NHEAD, (y + 1) * NHEAD)
        bias = jnp.where(my_y == y, own_bias, 0.0)
        stats = jnp.zeros((rows, HDIM), F32)
        for head in range(GROUP):
            cols = slice(head * HDIM, (head + 1) * HDIM)
            vcols = slice(WIDTH + head * HDIM, WIDTH + (head + 1) * HDIM)
            q = recv[blocks, 0 : 2 * TOK, cols].reshape(rows, HDIM)
            fresh = recv[blocks, 2 * TOK : BLOCK, cols].astype(F32).reshape(fresh_rows, HDIM).astype(BF16)
            fresh_v = jnp.dot(shift, fresh, preferred_element_type=F32).astype(BF16)
            s_own = nt_dot(q, own[:, cols]) + bias
            s_other = nt_dot(q, other[:, cols])
            s_fresh = nt_dot(q, fresh) + fresh_bias
            top = jnp.maximum(
                jnp.maximum(jnp.max(s_own, axis=1, keepdims=True), jnp.max(s_other, axis=1, keepdims=True)),
                jnp.max(s_fresh, axis=1, keepdims=True),
            )
            p_own = jnp.exp2((s_own - top) * SCALE2)
            p_other = jnp.exp2((s_other - top) * SCALE2)
            p_fresh = jnp.exp2((s_fresh - top) * SCALE2)
            total = (
                jnp.sum(p_own, axis=1, keepdims=True)
                + jnp.sum(p_other, axis=1, keepdims=True)
                + jnp.sum(p_fresh, axis=1, keepdims=True)
            )
            acc = jnp.dot(p_own.astype(BF16), own[:, vcols], preferred_element_type=F32)
            acc = acc + jnp.dot(p_other.astype(BF16), other[:, vcols], preferred_element_type=F32)
            acc = acc + jnp.dot(p_fresh.astype(BF16), fresh_v, preferred_element_type=F32)
            gate = jnp.where(step_of_row == 0, gate0[:, cols], gate1[:, cols])
            mixed = (acc / total) * gate
            out[blocks, :, cols] = mixed.astype(BF16).reshape(NHEAD, 2 * TOK, HDIM)
            size = top * SCALE2 + jnp.log(total) * (1.0 / LN2)
            for i, piece in enumerate(split3(size)):
                stats = jnp.where(lane == 3 * head + i, piece.astype(F32), stats)
        out[blocks, :, WIDTH:] = stats.astype(BF16).reshape(NHEAD, 2 * TOK, HDIM)


def merge_kernel(recv, out_first, out_second):
    rows = NHEAD * 2 * TOK
    at = lax.broadcasted_iota(jnp.int32, (HDIM, WIDTH), 0)
    to = lax.broadcasted_iota(jnp.int32, (HDIM, WIDTH), 1)
    spread = jnp.where(at // 3 == to // HDIM, 1.0, 0.0).astype(BF16)
    sizes, parts = [], []
    for y in range(NY):
        blocks = slice(y * NHEAD, (y + 1) * NHEAD)
        stats = recv[blocks, :, WIDTH:].reshape(rows, HDIM)
        sizes.append(jnp.dot(stats, spread, preferred_element_type=F32))
        parts.append(recv[blocks, :, 0:WIDTH].reshape(rows, WIDTH).astype(F32))
    top = functools.reduce(jnp.maximum, sizes)
    total = jnp.zeros_like(top)
    acc = jnp.zeros_like(top)
    for size, part in zip(sizes, parts, strict=True):
        weight = jnp.exp2(size - top)
        total = total + weight
        acc = acc + weight * part
    result = acc / total
    for g in range(NHEAD):
        cols = slice(g * WIDTH, (g + 1) * WIDTH)
        out_first[:, cols] = result[g * 2 * TOK : g * 2 * TOK + TOK].astype(BF16)
        out_second[:, cols] = result[g * 2 * TOK + TOK : (g + 1) * 2 * TOK].astype(BF16)


def vmem(n):
    return [pl.BlockSpec(memory_space=pltpu.VMEM)] * n


def smem(n):
    return [pl.BlockSpec(memory_space=pltpu.SMEM)] * n


PARAMS = pltpu.CompilerParams(vmem_limit_bytes=40 * 1024 * 1024)


def body(q1, k1, v1, q2, k2, v2, key_stale, value_stale, gate_table, step_index):
    shape = jax.ShapeDtypeStruct
    packed, kv = pl.pallas_call(
        pack_kernel,
        out_shape=(shape((PEERS, BLOCK, WIDTH), BF16), shape((PATCH, 2 * WIDTH), BF16)),
        in_specs=vmem(8),
        out_specs=tuple(vmem(2)),
        compiler_params=PARAMS,
        name="pack",
    )(q1, k1, v1, q2, k2, v2, key_stale, value_stale)
    recv = lax.all_to_all(packed, PLANE, split_axis=0, concat_axis=0, tiled=True)
    own = lax.all_gather(kv, "z", axis=0, tiled=True)
    other = lax.ppermute(own, "c", [(0, 1), (1, 0)])
    where = jnp.stack([lax.axis_index("z"), lax.axis_index("y")]).astype(jnp.int32)
    partial = pl.pallas_call(
        attend_kernel,
        out_shape=shape((PEERS, 2 * TOK, WIDTH + HDIM), BF16),
        in_specs=smem(2) + vmem(4),
        out_specs=vmem(1)[0],
        compiler_params=PARAMS,
        name="attend",
    )(where, step_index, recv, own, other, gate_table)
    back = lax.all_to_all(partial, PLANE, split_axis=0, concat_axis=0, tiled=True)
    return pl.pallas_call(
        merge_kernel,
        out_shape=(shape((TOK, NHEAD * WIDTH), BF16),) * 2,
        in_specs=vmem(1),
        out_specs=tuple(vmem(2)),
        compiler_params=PARAMS,
        name="merge",
    )(back)


def solution(mesh):
    fine = Mesh(mesh.devices.reshape(NZ, NY, NC, NH, NX), ("z", "y", "c", "h", "x"))
    tokens = P(("z", "y", "c", "h", "x"), None)
    kept = P(("z", "y", "c"), ("h", "x"))
    return jax.shard_map(
        body,
        mesh=fine,
        in_specs=(tokens,) * 6 + (kept, kept, P(None, ("h", "x")), P()),
        out_specs=(tokens, tokens),
        check_vma=False,
    )
```

```python
import functools

import jax
import jax.numpy as jnp
from jax import lax
from jax.experimental import pallas as pl
from jax.experimental.pallas import tpu as pltpu
from jax.sharding import Mesh
from jax.sharding import PartitionSpec as P

HDIM = 128
GROUP = 3
WIDTH = GROUP * HDIM
NZ, NY, NC, NH, NX = 8, 4, 2, 2, 4
NHEAD = NH * NX
PEERS = NY * NHEAD
TOK = 8
PATCH = TOK * NHEAD
FRESH = 2 * TOK // NY
BLOCK = 2 * TOK + 2 * FRESH
SENT = 2 * TOK * GROUP + TOK
SCALE2 = HDIM ** (-0.5) * 1.4426950408889634
LN2 = 0.6931471805599453
NEG = -1e30
F32 = jnp.float32
BF16 = jnp.bfloat16
PLANE = ("y", "h", "x")


def pack_kernel(q1, k1, v1, q2, k2, v2, ks, vs, out, kv, b0, b1, b2, b3, b4, b5, sems):
    pairs = [(q1, b0), (q2, b1), (k1, b2), (k2, b3), (v1, b4), (v2, b5)]
    pairs += [(ks, kv.at[:, 0:WIDTH]), (vs, kv.at[:, WIDTH : 2 * WIDTH])]
    copies = [pltpu.make_async_copy(src, dst, sems.at[i]) for i, (src, dst) in enumerate(pairs)]
    for copy in copies:
        copy.start()
    share = TOK // NY
    for copy in copies:
        copy.wait()
    for g in range(NHEAD):
        cols = slice(g * WIDTH, (g + 1) * WIDTH)
        queries = jnp.concatenate([b0[:, cols].astype(F32), b1[:, cols].astype(F32)], axis=0).astype(BF16)
        fresh = [ref[:, cols].astype(F32) for ref in (b2, b3, b4, b5)]
        for y in range(NY):
            rows = slice(y * share, (y + 1) * share)
            part = jnp.concatenate([f[rows] for f in fresh], axis=0).astype(BF16)
            out[y * NHEAD + g, 0 : 2 * TOK, :] = queries
            out[y * NHEAD + g, 2 * TOK : BLOCK, :] = part


def split3(x):
    hi = x.astype(BF16)
    rest = x - hi.astype(F32)
    mid = rest.astype(BF16)
    lo = (rest - mid.astype(F32)).astype(BF16)
    return hi, mid, lo


def nt_dot(a, b):
    return lax.dot_general(a, b, (((1,), (1,)), ((), ())), preferred_element_type=F32)


def attend_kernel(step_ref, recv, own, other, gates, out):
    my_z = lax.axis_index("z")
    my_y = lax.axis_index("y")
    keys = NZ * PATCH
    rows = 2 * PATCH
    fresh_rows = NHEAD * 2 * FRESH
    col = lax.broadcasted_iota(jnp.int32, (1, keys), 1)
    own_bias = jnp.where(col // PATCH == my_z, NEG, 0.0)
    q_step = (lax.broadcasted_iota(jnp.int32, (rows, fresh_rows), 0) // TOK) % 2
    f_kind = lax.broadcasted_iota(jnp.int32, (rows, fresh_rows), 1) % (2 * FRESH) // (FRESH // 2)
    fresh_bias = jnp.where(f_kind == q_step, 0.0, NEG)
    at = lax.broadcasted_iota(jnp.int32, (fresh_rows, fresh_rows), 0)
    to = lax.broadcasted_iota(jnp.int32, (fresh_rows, fresh_rows), 1)
    shift = jnp.where(to == at + FRESH, 1.0, 0.0).astype(BF16)
    gate0 = gates[pl.ds(step_ref[0], 1), :]
    gate1 = gates[pl.ds(step_ref[1], 1), :]
    lane = lax.broadcasted_iota(jnp.int32, (rows, HDIM), 1)
    step_of_row = (lax.broadcasted_iota(jnp.int32, (rows, HDIM), 0) // TOK) % 2
    slot = lane - 3 * GROUP * step_of_row
    stats = [jnp.zeros((rows, HDIM), F32) for _ in range(NY)]
    for head in range(GROUP):
        cols = slice(head * HDIM, (head + 1) * HDIM)
        vcols = slice(WIDTH + head * HDIM, WIDTH + (head + 1) * HDIM)
        q = recv[:, 0 : 2 * TOK, cols].reshape(NY * rows, HDIM)
        s_own = nt_dot(q, own[:, cols])
        s_other = nt_dot(q, other[:, cols])
        w_own, w_other, tops, totals, accs = [], [], [], [], []
        for y in range(NY):
            part = slice(y * rows, (y + 1) * rows)
            fresh = recv[y * NHEAD : (y + 1) * NHEAD, 2 * TOK : BLOCK, cols].astype(F32)
            fresh = fresh.reshape(fresh_rows, HDIM).astype(BF16)
            fresh_v = jnp.dot(shift, fresh, preferred_element_type=F32).astype(BF16)
            s_f = nt_dot(q[part], fresh) + fresh_bias
            s_a = s_own[part] + jnp.where(my_y == y, own_bias, 0.0)
            s_b = s_other[part]
            top = jnp.maximum(
                jnp.max(jnp.maximum(s_a, s_b), axis=1, keepdims=True), jnp.max(s_f, axis=1, keepdims=True)
            )
            p_a = jnp.exp2((s_a - top) * SCALE2)
            p_b = jnp.exp2((s_b - top) * SCALE2)
            p_f = jnp.exp2((s_f - top) * SCALE2)
            totals.append(jnp.sum(p_a + p_b, axis=1, keepdims=True) + jnp.sum(p_f, axis=1, keepdims=True))
            tops.append(top)
            w_own.append(p_a.astype(BF16))
            w_other.append(p_b.astype(BF16))
            accs.append(jnp.dot(p_f.astype(BF16), fresh_v, preferred_element_type=F32))
        acc = jnp.dot(jnp.concatenate(w_own, axis=0), own[:, vcols], preferred_element_type=F32)
        acc = acc + jnp.dot(jnp.concatenate(w_other, axis=0), other[:, vcols], preferred_element_type=F32)
        gate = jnp.where(step_of_row == 0, gate0[:, cols], gate1[:, cols])
        for y in range(NY):
            mixed = ((acc[y * rows : (y + 1) * rows] + accs[y]) / totals[y]) * gate
            out[y * NHEAD : (y + 1) * NHEAD, head * 2 * TOK : (head + 1) * 2 * TOK, :] = (
                mixed.astype(BF16).reshape(NHEAD, 2 * TOK, HDIM)
            )
            size = tops[y] * SCALE2 + jnp.log(totals[y]) * (1.0 / LN2)
            for i, piece in enumerate(split3(size)):
                stats[y] = jnp.where(slot == 3 * head + i, piece.astype(F32), stats[y])
    for y in range(NY):
        folded = jnp.sum(stats[y].reshape(NHEAD, 2, TOK, HDIM), axis=1)
        out[y * NHEAD : (y + 1) * NHEAD, SENT - TOK : SENT, :] = folded.astype(BF16)


def merge_kernel(recv, out_first, out_second):
    at = lax.broadcasted_iota(jnp.int32, (HDIM, 2 * WIDTH), 0)
    to = lax.broadcasted_iota(jnp.int32, (HDIM, 2 * WIDTH), 1)
    spread = jnp.where(at // 3 == to // HDIM, 1.0, 0.0).astype(BF16)
    sizes, parts = [], []
    for y in range(NY):
        blocks = slice(y * NHEAD, (y + 1) * NHEAD)
        stats = recv[blocks, SENT - TOK : SENT, :].astype(F32).reshape(NHEAD * TOK, HDIM).astype(BF16)
        sizes.append(jnp.dot(stats, spread, preferred_element_type=F32))
        parts.append(recv[blocks, 0 : SENT - TOK, :].astype(F32))
    for step, out in ((0, out_first), (1, out_second)):
        for head in range(GROUP):
            lanes = slice((step * GROUP + head) * HDIM, (step * GROUP + head + 1) * HDIM)
            rows = slice((2 * head + step) * TOK, (2 * head + step + 1) * TOK)
            size = [s[:, lanes] for s in sizes]
            top = functools.reduce(jnp.maximum, size)
            total = jnp.zeros_like(top)
            acc = jnp.zeros_like(top)
            for y in range(NY):
                weight = jnp.exp2(size[y] - top)
                total = total + weight
                acc = acc + weight * parts[y][:, rows, :].reshape(NHEAD * TOK, HDIM)
            result = (acc / total).astype(BF16)
            for g in range(NHEAD):
                cols = slice(g * WIDTH + head * HDIM, g * WIDTH + (head + 1) * HDIM)
                out[:, cols] = result[g * TOK : (g + 1) * TOK]


def vmem(n):
    return [pl.BlockSpec(memory_space=pltpu.VMEM)] * n


def smem(n):
    return [pl.BlockSpec(memory_space=pltpu.SMEM)] * n


PARAMS = pltpu.CompilerParams(vmem_limit_bytes=40 * 1024 * 1024)
PACK_PARAMS = pltpu.CompilerParams(vmem_limit_bytes=62 * 1024 * 1024)


def body(q1, k1, v1, q2, k2, v2, key_stale, value_stale, gate_table, step_index):
    shape = jax.ShapeDtypeStruct
    packed, kv = pl.pallas_call(
        pack_kernel,
        out_shape=(shape((PEERS, BLOCK, WIDTH), BF16), shape((PATCH, 2 * WIDTH), BF16)),
        in_specs=[pl.BlockSpec(memory_space=pltpu.HBM)] * 8,
        out_specs=tuple(vmem(2)),
        scratch_shapes=[pltpu.VMEM((TOK, NHEAD * WIDTH), BF16)] * 6 + [pltpu.SemaphoreType.DMA((8,))],
        compiler_params=PACK_PARAMS,
        name="pack",
    )(q1, k1, v1, q2, k2, v2, key_stale, value_stale)
    recv = lax.all_to_all(packed, PLANE, split_axis=0, concat_axis=0, tiled=True)
    own = lax.all_gather(kv, "z", axis=0, tiled=True)
    other = lax.ppermute(own, "c", [(0, 1), (1, 0)])
    partial = pl.pallas_call(
        attend_kernel,
        out_shape=shape((PEERS, SENT, HDIM), BF16),
        in_specs=smem(1) + vmem(4),
        out_specs=vmem(1)[0],
        compiler_params=PARAMS,
        name="attend",
    )(step_index, recv, own, other, gate_table)
    back = lax.all_to_all(partial, PLANE, split_axis=0, concat_axis=0, tiled=True)
    return pl.pallas_call(
        merge_kernel,
        out_shape=(shape((TOK, NHEAD * WIDTH), BF16),) * 2,
        in_specs=vmem(1),
        out_specs=tuple(vmem(2)),
        compiler_params=PARAMS,
        name="merge",
    )(back)


def solution(mesh):
    fine = Mesh(mesh.devices.reshape(NZ, NY, NC, NH, NX), ("z", "y", "c", "h", "x"))
    tokens = P(("z", "y", "c", "h", "x"), None)
    kept = P(("z", "y", "c"), ("h", "x"))
    return jax.shard_map(
        body,
        mesh=fine,
        in_specs=(tokens,) * 6 + (kept, kept, P(None, ("h", "x")), P()),
        out_specs=(tokens, tokens),
        check_vma=False,
    )
```

```python
import functools

import jax
import jax.numpy as jnp
from jax import lax
from jax.experimental import pallas as pl
from jax.experimental.pallas import tpu as pltpu
from jax.sharding import Mesh
from jax.sharding import PartitionSpec as P

HDIM = 128
GROUP = 3
WIDTH = GROUP * HDIM
NZ, NY, NC, NH, NX = 8, 4, 2, 2, 4
NHEAD = NH * NX
PEERS = NY * NHEAD
TOK = 8
PATCH = TOK * NHEAD
FRESH = 2 * TOK // NY
BLOCK = 2 * TOK + 2 * FRESH
SENT = 2 * TOK * GROUP + TOK
SCALE2 = HDIM ** (-0.5) * 1.4426950408889634
LN2 = 0.6931471805599453
NEG = -1e30
F32 = jnp.float32
BF16 = jnp.bfloat16
PLANE = ("y", "h", "x")


def pack_kernel(q1, k1, v1, q2, k2, v2, ks, vs, out, kv, b0, b1, b2, b3, b4, b5, sems):
    pairs = [(q1, b0), (q2, b1), (k1, b2), (k2, b3), (v1, b4), (v2, b5)]
    pairs += [(ks, kv.at[:, 0:WIDTH]), (vs, kv.at[:, WIDTH : 2 * WIDTH])]
    copies = [pltpu.make_async_copy(src, dst, sems.at[i]) for i, (src, dst) in enumerate(pairs)]
    for copy in copies:
        copy.start()
    share = TOK // NY
    for copy in copies:
        copy.wait()
    for g in range(NHEAD):
        cols = slice(g * WIDTH, (g + 1) * WIDTH)
        queries = jnp.concatenate([b0[:, cols].astype(F32), b1[:, cols].astype(F32)], axis=0).astype(BF16)
        fresh = [ref[:, cols].astype(F32) for ref in (b2, b3, b4, b5)]
        for y in range(NY):
            rows = slice(y * share, (y + 1) * share)
            part = jnp.concatenate([f[rows] for f in fresh], axis=0).astype(BF16)
            out[y * NHEAD + g, 0 : 2 * TOK, :] = queries
            out[y * NHEAD + g, 2 * TOK : BLOCK, :] = part


def split3(x):
    hi = x.astype(BF16)
    rest = x - hi.astype(F32)
    mid = rest.astype(BF16)
    lo = (rest - mid.astype(F32)).astype(BF16)
    return hi, mid, lo


def nt_dot(a, b):
    return lax.dot_general(a, b, (((1,), (1,)), ((), ())), preferred_element_type=F32)


def attend_kernel(step_ref, recv, own, other, gates, out):
    mine = 2 * lax.axis_index("zq")
    my_y = lax.axis_index("y")
    keys = NZ * PATCH
    rows = 2 * PATCH
    fresh_rows = NHEAD * 2 * FRESH
    col = lax.broadcasted_iota(jnp.int32, (1, keys), 1)
    own_bias = jnp.where(col // PATCH == mine, NEG, 0.0)
    q_step = (lax.broadcasted_iota(jnp.int32, (rows, fresh_rows), 0) // TOK) % 2
    f_kind = lax.broadcasted_iota(jnp.int32, (rows, fresh_rows), 1) % (2 * FRESH) // (FRESH // 2)
    fresh_bias = jnp.where(f_kind == q_step, 0.0, NEG)
    at = lax.broadcasted_iota(jnp.int32, (fresh_rows, fresh_rows), 0)
    to = lax.broadcasted_iota(jnp.int32, (fresh_rows, fresh_rows), 1)
    shift = jnp.where(to == at + FRESH, 1.0, 0.0).astype(BF16)
    gate0 = gates[pl.ds(step_ref[0], 1), :]
    gate1 = gates[pl.ds(step_ref[1], 1), :]
    lane = lax.broadcasted_iota(jnp.int32, (rows, HDIM), 1)
    step_of_row = (lax.broadcasted_iota(jnp.int32, (rows, HDIM), 0) // TOK) % 2
    slot = lane - 3 * GROUP * step_of_row
    stats = [jnp.zeros((rows, HDIM), F32) for _ in range(NY)]

    def scores(head):
        cols = slice(head * HDIM, (head + 1) * HDIM)
        q = recv[:, 0 : 2 * TOK, cols].reshape(NY * rows, HDIM)
        extra = []
        for y in range(NY):
            fresh = recv[y * NHEAD : (y + 1) * NHEAD, 2 * TOK : BLOCK, cols].astype(F32)
            fresh = fresh.reshape(fresh_rows, HDIM).astype(BF16)
            fresh_v = jnp.dot(shift, fresh, preferred_element_type=F32).astype(BF16)
            extra.append((nt_dot(q[y * rows : (y + 1) * rows], fresh) + fresh_bias, fresh_v))
        return nt_dot(q, own[:, cols]), nt_dot(q, other[:, cols]), extra

    ready = scores(0)
    for head in range(GROUP):
        vcols = slice(WIDTH + head * HDIM, WIDTH + (head + 1) * HDIM)
        s_own, s_other, extra = ready
        if head + 1 < GROUP:
            ready = scores(head + 1)
        w_own, w_other, tops, totals, accs = [], [], [], [], []
        for y in range(NY):
            part = slice(y * rows, (y + 1) * rows)
            s_a = s_own[part] + jnp.where(my_y == y, own_bias, 0.0)
            s_b = s_other[part]
            s_f, fresh_v = extra[y]
            top = jnp.maximum(
                jnp.max(jnp.maximum(s_a, s_b), axis=1, keepdims=True), jnp.max(s_f, axis=1, keepdims=True)
            )
            p_a = jnp.exp2((s_a - top) * SCALE2)
            p_b = jnp.exp2((s_b - top) * SCALE2)
            p_f = jnp.exp2((s_f - top) * SCALE2)
            totals.append(jnp.sum(p_a + p_b, axis=1, keepdims=True) + jnp.sum(p_f, axis=1, keepdims=True))
            tops.append(top)
            w_own.append(p_a.astype(BF16))
            w_other.append(p_b.astype(BF16))
            accs.append(jnp.dot(p_f.astype(BF16), fresh_v, preferred_element_type=F32))
        acc = jnp.dot(jnp.concatenate(w_own, axis=0), own[:, vcols], preferred_element_type=F32)
        acc = acc + jnp.dot(jnp.concatenate(w_other, axis=0), other[:, vcols], preferred_element_type=F32)
        cols = slice(head * HDIM, (head + 1) * HDIM)
        gate = jnp.where(step_of_row == 0, gate0[:, cols], gate1[:, cols])
        for y in range(NY):
            mixed = ((acc[y * rows : (y + 1) * rows] + accs[y]) / totals[y]) * gate
            out[y * NHEAD : (y + 1) * NHEAD, head * 2 * TOK : (head + 1) * 2 * TOK, :] = (
                mixed.astype(BF16).reshape(NHEAD, 2 * TOK, HDIM)
            )
            size = tops[y] * SCALE2 + jnp.log(totals[y]) * (1.0 / LN2)
            for i, piece in enumerate(split3(size)):
                stats[y] = jnp.where(slot == 3 * head + i, piece.astype(F32), stats[y])
    for y in range(NY):
        folded = jnp.sum(stats[y].reshape(NHEAD, 2, TOK, HDIM), axis=1)
        out[y * NHEAD : (y + 1) * NHEAD, SENT - TOK : SENT, :] = folded.astype(BF16)


def merge_kernel(recv, out_first, out_second):
    at = lax.broadcasted_iota(jnp.int32, (HDIM, 2 * WIDTH), 0)
    to = lax.broadcasted_iota(jnp.int32, (HDIM, 2 * WIDTH), 1)
    spread = jnp.where(at // 3 == to // HDIM, 1.0, 0.0).astype(BF16)
    sizes, parts = [], []
    for y in range(NY):
        blocks = slice(y * NHEAD, (y + 1) * NHEAD)
        stats = recv[blocks, SENT - TOK : SENT, :].astype(F32).reshape(NHEAD * TOK, HDIM).astype(BF16)
        sizes.append(jnp.dot(stats, spread, preferred_element_type=F32))
        parts.append(recv[blocks, 0 : SENT - TOK, :].astype(F32))
    for step, out in ((0, out_first), (1, out_second)):
        for head in range(GROUP):
            lanes = slice((step * GROUP + head) * HDIM, (step * GROUP + head + 1) * HDIM)
            rows = slice((2 * head + step) * TOK, (2 * head + step + 1) * TOK)
            size = [s[:, lanes] for s in sizes]
            top = functools.reduce(jnp.maximum, size)
            total = jnp.zeros_like(top)
            acc = jnp.zeros_like(top)
            for y in range(NY):
                weight = jnp.exp2(size[y] - top)
                total = total + weight
                acc = acc + weight * parts[y][:, rows, :].reshape(NHEAD * TOK, HDIM)
            result = (acc / total).astype(BF16)
            for g in range(NHEAD):
                cols = slice(g * WIDTH + head * HDIM, g * WIDTH + (head + 1) * HDIM)
                out[:, cols] = result[g * TOK : (g + 1) * TOK]


def vmem(n):
    return [pl.BlockSpec(memory_space=pltpu.VMEM)] * n


def smem(n):
    return [pl.BlockSpec(memory_space=pltpu.SMEM)] * n


PARAMS = pltpu.CompilerParams(vmem_limit_bytes=40 * 1024 * 1024)
PACK_PARAMS = pltpu.CompilerParams(vmem_limit_bytes=62 * 1024 * 1024)


def body(q1, k1, v1, q2, k2, v2, key_stale, value_stale, gate_table, step_index):
    shape = jax.ShapeDtypeStruct
    packed, kv = pl.pallas_call(
        pack_kernel,
        out_shape=(shape((PEERS, BLOCK, WIDTH), BF16), shape((PATCH, 2 * WIDTH), BF16)),
        in_specs=[pl.BlockSpec(memory_space=pltpu.HBM)] * 8,
        out_specs=tuple(vmem(2)),
        scratch_shapes=[pltpu.VMEM((TOK, NHEAD * WIDTH), BF16)] * 6 + [pltpu.SemaphoreType.DMA((8,))],
        compiler_params=PACK_PARAMS,
        name="pack",
    )(q1, k1, v1, q2, k2, v2, key_stale, value_stale)
    recv = lax.all_to_all(packed, PLANE, split_axis=0, concat_axis=0, tiled=True)
    pair = lax.ppermute(kv, "zp", [(0, 1), (1, 0)])
    own = lax.all_gather(jnp.concatenate([kv, pair], axis=0), "zq", axis=0, tiled=True)
    other = lax.ppermute(own, "c", [(0, 1), (1, 0)])
    partial = pl.pallas_call(
        attend_kernel,
        out_shape=shape((PEERS, SENT, HDIM), BF16),
        in_specs=smem(1) + vmem(4),
        out_specs=vmem(1)[0],
        compiler_params=PARAMS,
        name="attend",
    )(step_index, recv, own, other, gate_table)
    back = lax.all_to_all(partial, PLANE, split_axis=0, concat_axis=0, tiled=True)
    return pl.pallas_call(
        merge_kernel,
        out_shape=(shape((TOK, NHEAD * WIDTH), BF16),) * 2,
        in_specs=vmem(1),
        out_specs=tuple(vmem(2)),
        compiler_params=PARAMS,
        name="merge",
    )(back)


def solution(mesh):
    fine = Mesh(mesh.devices.reshape(NZ // 2, 2, NY, NC, NH, NX), ("zq", "zp", "y", "c", "h", "x"))
    tokens = P(("zq", "zp", "y", "c", "h", "x"), None)
    kept = P(("zq", "zp", "y", "c"), ("h", "x"))
    return jax.shard_map(
        body,
        mesh=fine,
        in_specs=(tokens,) * 6 + (kept, kept, P(None, ("h", "x")), P()),
        out_specs=(tokens, tokens),
        check_vma=False,
    )
```

```python
import functools

import jax
import jax.numpy as jnp
from jax import lax
from jax.experimental import pallas as pl
from jax.experimental.pallas import tpu as pltpu
from jax.sharding import Mesh
from jax.sharding import PartitionSpec as P

HDIM = 128
GROUP = 3
WIDTH = GROUP * HDIM
NZ, NY, NC, NH, NX = 8, 4, 2, 2, 4
NHEAD = NH * NX
PEERS = NY * NHEAD
TOK = 8
PATCH = TOK * NHEAD
FRESH = 2 * TOK // NY
BLOCK = 2 * TOK + 2 * FRESH
SENT = 2 * TOK * GROUP + TOK
SCALE2 = HDIM ** (-0.5) * 1.4426950408889634
LN2 = 0.6931471805599453
NEG = -1e30
F32 = jnp.float32
BF16 = jnp.bfloat16
PLANE = ("y", "h", "x")


def pack_kernel(q1, k1, v1, q2, k2, v2, ks, vs, out, kv, b0, b1, b2, b3, b4, b5, sems):
    pairs = [(q1, b0), (q2, b1), (k1, b2), (k2, b3), (v1, b4), (v2, b5)]
    pairs += [(ks, kv.at[:, 0:WIDTH]), (vs, kv.at[:, WIDTH : 2 * WIDTH])]
    copies = [pltpu.make_async_copy(src, dst, sems.at[i]) for i, (src, dst) in enumerate(pairs)]
    for copy in copies:
        copy.start()
    share = TOK // NY
    for copy in copies:
        copy.wait()
    for g in range(NHEAD):
        cols = slice(g * WIDTH, (g + 1) * WIDTH)
        queries = jnp.concatenate([b0[:, cols].astype(F32), b1[:, cols].astype(F32)], axis=0).astype(BF16)
        fresh = [ref[:, cols].astype(F32) for ref in (b2, b3, b4, b5)]
        for y in range(NY):
            rows = slice(y * share, (y + 1) * share)
            part = jnp.concatenate([f[rows] for f in fresh], axis=0).astype(BF16)
            out[y * NHEAD + g, 0 : 2 * TOK, :] = queries
            out[y * NHEAD + g, 2 * TOK : BLOCK, :] = part


def split3(x):
    hi = x.astype(BF16)
    rest = x - hi.astype(F32)
    mid = rest.astype(BF16)
    lo = (rest - mid.astype(F32)).astype(BF16)
    return hi, mid, lo


def nt_dot(a, b):
    return lax.dot_general(a, b, (((1,), (1,)), ((), ())), preferred_element_type=F32)


ROWS = 2 * PATCH
ALL = NY * ROWS
FRESH_ROWS = NHEAD * 2 * FRESH
KEYS = NZ * PATCH


def head_cols(head):
    return slice(head * HDIM, (head + 1) * HDIM)


def value_cols(head):
    return slice(WIDTH + head * HDIM, WIDTH + (head + 1) * HDIM)


def queries_of(recv, head):
    return recv[:, 0 : 2 * TOK, head_cols(head)].reshape(ALL, HDIM)


def patch_rows(y):
    return slice(y * ROWS, (y + 1) * ROWS)


def row_max(x):
    return jnp.max(x, axis=1, keepdims=True)


def row_sum(x):
    return jnp.sum(x, axis=1, keepdims=True)


def attend_own_kernel(step_ref, recv, own, gates, acc_out, top_out, total_out, gate_out):
    mine = 2 * lax.axis_index("zq")
    my_y = lax.axis_index("y")
    col = lax.broadcasted_iota(jnp.int32, (1, KEYS), 1)
    own_bias = jnp.where(col // PATCH == mine, NEG, 0.0)
    q_step = (lax.broadcasted_iota(jnp.int32, (ROWS, FRESH_ROWS), 0) // TOK) % 2
    f_kind = lax.broadcasted_iota(jnp.int32, (ROWS, FRESH_ROWS), 1) % (2 * FRESH) // (FRESH // 2)
    fresh_bias = jnp.where(f_kind == q_step, 0.0, NEG)
    at = lax.broadcasted_iota(jnp.int32, (FRESH_ROWS, FRESH_ROWS), 0)
    to = lax.broadcasted_iota(jnp.int32, (FRESH_ROWS, FRESH_ROWS), 1)
    shift = jnp.where(to == at + FRESH, 1.0, 0.0).astype(BF16)
    for step in range(2):
        gate = gates[pl.ds(step_ref[step], 1), :]
        gate_out[step * TOK : (step + 1) * TOK, :] = jnp.broadcast_to(gate, (TOK, WIDTH))

    def scores(head):
        q = queries_of(recv, head)
        extra = []
        for y in range(NY):
            fresh = recv[y * NHEAD : (y + 1) * NHEAD, 2 * TOK : BLOCK, head_cols(head)].astype(F32)
            fresh = fresh.reshape(FRESH_ROWS, HDIM).astype(BF16)
            fresh_v = jnp.dot(shift, fresh, preferred_element_type=F32).astype(BF16)
            extra.append((nt_dot(q[patch_rows(y)], fresh) + fresh_bias, fresh_v))
        return nt_dot(q, own[:, head_cols(head)]), extra

    ready = scores(0)
    for head in range(GROUP):
        s_own, extra = ready
        if head + 1 < GROUP:
            ready = scores(head + 1)
        weights, accs = [], []
        for y in range(NY):
            s_a = s_own[patch_rows(y)] + jnp.where(my_y == y, own_bias, 0.0)
            s_f, fresh_v = extra[y]
            top = jnp.maximum(row_max(s_a), row_max(s_f))
            p_a = jnp.exp2((s_a - top) * SCALE2)
            p_f = jnp.exp2((s_f - top) * SCALE2)
            total = row_sum(p_a) + row_sum(p_f)
            weights.append(p_a.astype(BF16))
            accs.append(jnp.dot(p_f.astype(BF16), fresh_v, preferred_element_type=F32))
            top_out[patch_rows(y), head_cols(head)] = jnp.broadcast_to(top, (ROWS, HDIM))
            total_out[patch_rows(y), head_cols(head)] = jnp.broadcast_to(total, (ROWS, HDIM))
        acc = jnp.dot(jnp.concatenate(weights, axis=0), own[:, value_cols(head)], preferred_element_type=F32)
        acc_out[:, head_cols(head)] = acc + jnp.concatenate(accs, axis=0)


def attend_other_kernel(recv, other, acc_in, top_in, total_in, gate_in, out):
    lane = lax.broadcasted_iota(jnp.int32, (ROWS, HDIM), 1)
    step_of_row = (lax.broadcasted_iota(jnp.int32, (ROWS, HDIM), 0) // TOK) % 2
    slot = lane - 3 * GROUP * step_of_row
    stats = [jnp.zeros((ROWS, HDIM), F32) for _ in range(NY)]

    def scores(head):
        return nt_dot(queries_of(recv, head), other[:, head_cols(head)])

    ready = scores(0)
    for head in range(GROUP):
        s_all = ready
        if head + 1 < GROUP:
            ready = scores(head + 1)
        weights, tops, totals, keeps = [], [], [], []
        for y in range(NY):
            s_b = s_all[patch_rows(y)]
            old_top = top_in[patch_rows(y), head_cols(head)]
            top = jnp.maximum(jnp.broadcast_to(row_max(s_b), (ROWS, HDIM)), old_top)
            p_b = jnp.exp2((s_b - jnp.concatenate([top] * (KEYS // HDIM), axis=1)) * SCALE2)
            keep = jnp.exp2((old_top - top) * SCALE2)
            tops.append(top)
            keeps.append(keep)
            totals.append(jnp.broadcast_to(row_sum(p_b), (ROWS, HDIM)) + keep * total_in[patch_rows(y), head_cols(head)])
            weights.append(p_b.astype(BF16))
        acc = jnp.dot(jnp.concatenate(weights, axis=0), other[:, value_cols(head)], preferred_element_type=F32)
        cols = head_cols(head)
        gate = jnp.concatenate([gate_in[:, cols]] * NHEAD, axis=0)
        for y in range(NY):
            total = acc[patch_rows(y)] + keeps[y] * acc_in[patch_rows(y), cols]
            mixed = (total / totals[y]) * gate
            out[y * NHEAD : (y + 1) * NHEAD, head * 2 * TOK : (head + 1) * 2 * TOK, :] = (
                mixed.astype(BF16).reshape(NHEAD, 2 * TOK, HDIM)
            )
            size = tops[y] * SCALE2 + jnp.log(totals[y]) * (1.0 / LN2)
            for i, piece in enumerate(split3(size)):
                stats[y] = jnp.where(slot == 3 * head + i, piece.astype(F32), stats[y])
    for y in range(NY):
        folded = jnp.sum(stats[y].reshape(NHEAD, 2, TOK, HDIM), axis=1)
        out[y * NHEAD : (y + 1) * NHEAD, SENT - TOK : SENT, :] = folded.astype(BF16)


def merge_kernel(recv, out_first, out_second):
    at = lax.broadcasted_iota(jnp.int32, (HDIM, 2 * WIDTH), 0)
    to = lax.broadcasted_iota(jnp.int32, (HDIM, 2 * WIDTH), 1)
    spread = jnp.where(at // 3 == to // HDIM, 1.0, 0.0).astype(BF16)
    sizes, parts = [], []
    for y in range(NY):
        blocks = slice(y * NHEAD, (y + 1) * NHEAD)
        stats = recv[blocks, SENT - TOK : SENT, :].astype(F32).reshape(NHEAD * TOK, HDIM).astype(BF16)
        sizes.append(jnp.dot(stats, spread, preferred_element_type=F32))
        parts.append(recv[blocks, 0 : SENT - TOK, :].astype(F32))
    for step, out in ((0, out_first), (1, out_second)):
        for head in range(GROUP):
            lanes = slice((step * GROUP + head) * HDIM, (step * GROUP + head + 1) * HDIM)
            rows = slice((2 * head + step) * TOK, (2 * head + step + 1) * TOK)
            size = [s[:, lanes] for s in sizes]
            top = functools.reduce(jnp.maximum, size)
            total = jnp.zeros_like(top)
            acc = jnp.zeros_like(top)
            for y in range(NY):
                weight = jnp.exp2(size[y] - top)
                total = total + weight
                acc = acc + weight * parts[y][:, rows, :].reshape(NHEAD * TOK, HDIM)
            result = (acc / total).astype(BF16)
            for g in range(NHEAD):
                cols = slice(g * WIDTH + head * HDIM, g * WIDTH + (head + 1) * HDIM)
                out[:, cols] = result[g * TOK : (g + 1) * TOK]


def vmem(n):
    return [pl.BlockSpec(memory_space=pltpu.VMEM)] * n


def smem(n):
    return [pl.BlockSpec(memory_space=pltpu.SMEM)] * n


PARAMS = pltpu.CompilerParams(vmem_limit_bytes=40 * 1024 * 1024)
PACK_PARAMS = pltpu.CompilerParams(vmem_limit_bytes=62 * 1024 * 1024)


def body(q1, k1, v1, q2, k2, v2, key_stale, value_stale, gate_table, step_index):
    shape = jax.ShapeDtypeStruct
    packed, kv = pl.pallas_call(
        pack_kernel,
        out_shape=(shape((PEERS, BLOCK, WIDTH), BF16), shape((PATCH, 2 * WIDTH), BF16)),
        in_specs=[pl.BlockSpec(memory_space=pltpu.HBM)] * 8,
        out_specs=tuple(vmem(2)),
        scratch_shapes=[pltpu.VMEM((TOK, NHEAD * WIDTH), BF16)] * 6 + [pltpu.SemaphoreType.DMA((8,))],
        compiler_params=PACK_PARAMS,
        name="pack",
    )(q1, k1, v1, q2, k2, v2, key_stale, value_stale)
    recv = lax.all_to_all(packed, PLANE, split_axis=0, concat_axis=0, tiled=True)
    pair = lax.ppermute(kv, "zp", [(0, 1), (1, 0)])
    own = lax.all_gather(jnp.concatenate([kv, pair], axis=0), "zq", axis=0, tiled=True)
    other = lax.ppermute(own, "c", [(0, 1), (1, 0)])
    cost = pl.CostEstimate(flops=4 * ALL * KEYS * WIDTH, bytes_accessed=2 << 20, transcendentals=GROUP * ALL * KEYS)
    state = (shape((ALL, WIDTH), F32),) * 3 + (shape((2 * TOK, WIDTH), F32),)
    state = pl.pallas_call(
        attend_own_kernel,
        out_shape=state,
        in_specs=smem(1) + vmem(3),
        out_specs=tuple(vmem(4)),
        compiler_params=PARAMS,
        cost_estimate=cost,
        name="attend_own",
    )(step_index, recv, own, gate_table)
    partial = pl.pallas_call(
        attend_other_kernel,
        out_shape=shape((PEERS, SENT, HDIM), BF16),
        in_specs=vmem(6),
        out_specs=vmem(1)[0],
        compiler_params=PARAMS,
        cost_estimate=cost,
        name="attend_other",
    )(recv, other, *state)
    back = lax.all_to_all(partial, PLANE, split_axis=0, concat_axis=0, tiled=True)
    return pl.pallas_call(
        merge_kernel,
        out_shape=(shape((TOK, NHEAD * WIDTH), BF16),) * 2,
        in_specs=vmem(1),
        out_specs=tuple(vmem(2)),
        compiler_params=PARAMS,
        name="merge",
    )(back)


def solution(mesh):
    fine = Mesh(mesh.devices.reshape(NZ // 2, 2, NY, NC, NH, NX), ("zq", "zp", "y", "c", "h", "x"))
    tokens = P(("zq", "zp", "y", "c", "h", "x"), None)
    kept = P(("zq", "zp", "y", "c"), ("h", "x"))
    return jax.shard_map(
        body,
        mesh=fine,
        in_specs=(tokens,) * 6 + (kept, kept, P(None, ("h", "x")), P()),
        out_specs=(tokens, tokens),
        check_vma=False,
    )
```

```python
import functools

import jax
import jax.numpy as jnp
from jax import lax
from jax.experimental import pallas as pl
from jax.experimental.pallas import tpu as pltpu
from jax.sharding import Mesh
from jax.sharding import PartitionSpec as P

HDIM = 128
GROUP = 3
WIDTH = GROUP * HDIM
NZ, NY, NC, NH, NX = 8, 4, 2, 2, 4
NHEAD = NH * NX
PEERS = NY * NHEAD
TOK = 8
PATCH = TOK * NHEAD
FRESH = 2 * TOK // NY
BLOCK = 2 * TOK + 2 * FRESH
SENT = TOK * GROUP + 1
SCALE2 = HDIM ** (-0.5) * 1.4426950408889634
LN2 = 0.6931471805599453
NEG = -1e30
F32 = jnp.float32
BF16 = jnp.bfloat16
PLANE = ("y", "h", "x")


def pack_kernel(q1, k1, v1, q2, k2, v2, ks, vs, out, kv, b0, b1, b2, b3, b4, b5, sems):
    pairs = [(q1, b0), (q2, b1), (k1, b2), (k2, b3), (v1, b4), (v2, b5)]
    pairs += [(ks, kv.at[:, 0:WIDTH]), (vs, kv.at[:, WIDTH : 2 * WIDTH])]
    copies = [pltpu.make_async_copy(src, dst, sems.at[i]) for i, (src, dst) in enumerate(pairs)]
    for copy in copies:
        copy.start()
    share = TOK // NY
    for copy in copies:
        copy.wait()
    for g in range(NHEAD):
        cols = slice(g * WIDTH, (g + 1) * WIDTH)
        queries = jnp.concatenate([b0[:, cols].astype(F32), b1[:, cols].astype(F32)], axis=0).astype(BF16)
        fresh = [ref[:, cols].astype(F32) for ref in (b2, b3, b4, b5)]
        for y in range(NY):
            rows = slice(y * share, (y + 1) * share)
            part = jnp.concatenate([f[rows] for f in fresh], axis=0).astype(BF16)
            out[y * NHEAD + g, 0 : 2 * TOK, :] = queries
            out[y * NHEAD + g, 2 * TOK : BLOCK, :] = part


def split3(x):
    hi = x.astype(BF16)
    rest = x - hi.astype(F32)
    mid = rest.astype(BF16)
    lo = (rest - mid.astype(F32)).astype(BF16)
    return hi, mid, lo


def nt_dot(a, b):
    return lax.dot_general(a, b, (((1,), (1,)), ((), ())), preferred_element_type=F32)


ROWS = 2 * PATCH
ALL = NY * ROWS
FRESH_ROWS = NHEAD * 2 * FRESH
KEYS = NZ * PATCH


def head_cols(head):
    return slice(head * HDIM, (head + 1) * HDIM)


def value_cols(head):
    return slice(WIDTH + head * HDIM, WIDTH + (head + 1) * HDIM)


def queries_of(recv, head):
    return recv[:, 0 : 2 * TOK, head_cols(head)].reshape(ALL, HDIM)


def patch_rows(y):
    return slice(y * ROWS, (y + 1) * ROWS)


def row_max(x):
    return jnp.max(x, axis=1, keepdims=True)


def row_sum(x):
    return jnp.sum(x, axis=1, keepdims=True)


def attend_own_kernel(step_ref, recv, own, gates, acc_out, top_out, total_out, gate_out):
    mine = 2 * lax.axis_index("zq")
    my_y = lax.axis_index("y")
    col = lax.broadcasted_iota(jnp.int32, (1, KEYS), 1)
    own_bias = jnp.where(col // PATCH == mine, NEG, 0.0)
    q_step = (lax.broadcasted_iota(jnp.int32, (ROWS, FRESH_ROWS), 0) // TOK) % 2
    f_kind = lax.broadcasted_iota(jnp.int32, (ROWS, FRESH_ROWS), 1) % (2 * FRESH) // (FRESH // 2)
    fresh_bias = jnp.where(f_kind == q_step, 0.0, NEG)
    at = lax.broadcasted_iota(jnp.int32, (FRESH_ROWS, FRESH_ROWS), 0)
    to = lax.broadcasted_iota(jnp.int32, (FRESH_ROWS, FRESH_ROWS), 1)
    shift = jnp.where(to == at + FRESH, 1.0, 0.0).astype(BF16)
    for step in range(2):
        gate = gates[pl.ds(step_ref[step], 1), :]
        gate_out[step * TOK : (step + 1) * TOK, :] = jnp.broadcast_to(gate, (TOK, WIDTH))

    def scores(head):
        q = queries_of(recv, head)
        extra = []
        for y in range(NY):
            fresh = recv[y * NHEAD : (y + 1) * NHEAD, 2 * TOK : BLOCK, head_cols(head)].astype(F32)
            fresh = fresh.reshape(FRESH_ROWS, HDIM).astype(BF16)
            fresh_v = jnp.dot(shift, fresh, preferred_element_type=F32).astype(BF16)
            extra.append((nt_dot(q[patch_rows(y)], fresh) + fresh_bias, fresh_v))
        return nt_dot(q, own[:, head_cols(head)]), extra

    ready = scores(0)
    for head in range(GROUP):
        s_own, extra = ready
        if head + 1 < GROUP:
            ready = scores(head + 1)
        weights, accs = [], []
        for y in range(NY):
            s_a = s_own[patch_rows(y)] + jnp.where(my_y == y, own_bias, 0.0)
            s_f, fresh_v = extra[y]
            top = jnp.maximum(row_max(s_a), row_max(s_f))
            p_a = jnp.exp2((s_a - top) * SCALE2)
            p_f = jnp.exp2((s_f - top) * SCALE2)
            total = row_sum(p_a) + row_sum(p_f)
            weights.append(p_a.astype(BF16))
            accs.append(jnp.dot(p_f.astype(BF16), fresh_v, preferred_element_type=F32))
            top_out[patch_rows(y), head_cols(head)] = jnp.broadcast_to(top, (ROWS, HDIM))
            total_out[patch_rows(y), head_cols(head)] = jnp.broadcast_to(total, (ROWS, HDIM))
        acc = jnp.dot(jnp.concatenate(weights, axis=0), own[:, value_cols(head)], preferred_element_type=F32)
        acc_out[:, head_cols(head)] = acc + jnp.concatenate(accs, axis=0)


def fold_matrix(height, width, short, long):
    at = lax.broadcasted_iota(jnp.int32, (height, width), short)
    row = lax.broadcasted_iota(jnp.int32, (height, width), long)
    return jnp.where(at == 2 * (row // (2 * TOK)) + row % 2, 1.0, 0.0).astype(BF16)


def attend_other_kernel(recv, other, acc_in, top_in, total_in, gate_in, out):
    lane = lax.broadcasted_iota(jnp.int32, (ROWS, HDIM), 1)
    slot = lane - 3 * GROUP * (lax.broadcasted_iota(jnp.int32, (ROWS, HDIM), 0) // 2 % TOK)
    stats = [jnp.zeros((ROWS, HDIM), F32) for _ in range(NY)]

    def scores(head):
        return nt_dot(queries_of(recv, head), other[:, head_cols(head)])

    ready = scores(0)
    for head in range(GROUP):
        s_all = ready
        if head + 1 < GROUP:
            ready = scores(head + 1)
        weights, tops, totals, keeps = [], [], [], []
        for y in range(NY):
            s_b = s_all[patch_rows(y)]
            old_top = top_in[patch_rows(y), head_cols(head)]
            top = jnp.maximum(jnp.broadcast_to(row_max(s_b), (ROWS, HDIM)), old_top)
            p_b = jnp.exp2((s_b - jnp.concatenate([top] * (KEYS // HDIM), axis=1)) * SCALE2)
            keep = jnp.exp2((old_top - top) * SCALE2)
            tops.append(top)
            keeps.append(keep)
            totals.append(jnp.broadcast_to(row_sum(p_b), (ROWS, HDIM)) + keep * total_in[patch_rows(y), head_cols(head)])
            weights.append(p_b.astype(BF16))
        acc = jnp.dot(jnp.concatenate(weights, axis=0), other[:, value_cols(head)], preferred_element_type=F32)
        cols = head_cols(head)
        gate = jnp.concatenate([gate_in[:, cols]] * NHEAD, axis=0)
        for y in range(NY):
            total = acc[patch_rows(y)] + keeps[y] * acc_in[patch_rows(y), cols]
            mixed = (total / totals[y]) * gate
            mixed = mixed.astype(BF16)
            for i in range(NHEAD):
                start = 2 * SENT * (i * NY + y) + 2 * TOK * head
                out[start : start + 2 * TOK, :] = mixed[2 * TOK * i : 2 * TOK * (i + 1)]
            size = tops[y] * SCALE2 + jnp.log(totals[y]) * (1.0 / LN2)
            for i, piece in enumerate(split3(size)):
                stats[y] = jnp.where(slot == 3 * head + i, piece.astype(F32), stats[y])
    for y in range(NY):
        for i in range(NHEAD):
            rows = stats[y][2 * TOK * i : 2 * TOK * i + TOK] + stats[y][2 * TOK * i + TOK : 2 * TOK * (i + 1)]
            rows = rows + pltpu.roll(rows, 4, 0)
            rows = rows + pltpu.roll(rows, 2, 0)
            start = 2 * SENT * (i * NY + y) + 2 * TOK * GROUP
            out[start : start + 2, :] = rows[0:2].astype(BF16)


def merge_kernel(recv, out_first, out_second):
    at = lax.broadcasted_iota(jnp.int32, (HDIM, WIDTH), 0)
    to = lax.broadcasted_iota(jnp.int32, (HDIM, WIDTH), 1)
    spread = jnp.where((at % (3 * GROUP)) // 3 == to // HDIM, 1.0, 0.0).astype(BF16)
    lane = lax.broadcasted_iota(jnp.int32, (ALL, HDIM), 1)
    pair = lax.broadcasted_iota(jnp.int32, (ALL, HDIM), 0) // 2 % TOK
    stats = jnp.concatenate(
        [recv[pl.ds(2 * SENT * (i * NY + y + 1) - 2, 2), :] for y in range(NY) for i in range(NHEAD)], axis=0
    )
    stats = jnp.dot(fold_matrix(ALL, 2 * PEERS, 1, 0), stats, preferred_element_type=F32)
    stats = jnp.where(lane // (3 * GROUP) == pair, stats, 0.0).astype(BF16)
    sizes = jnp.dot(stats, spread, preferred_element_type=F32)
    for head in range(GROUP):
        size = [sizes[patch_rows(y), head_cols(head)] for y in range(NY)]
        top = functools.reduce(jnp.maximum, size)
        total = jnp.zeros_like(top)
        acc = jnp.zeros_like(top)
        for y in range(NY):
            weight = jnp.exp2(size[y] - top)
            total = total + weight
            starts = [2 * SENT * (i * NY + y) + 2 * TOK * head for i in range(NHEAD)]
            part = jnp.concatenate([recv[a : a + 2 * TOK, :] for a in starts], axis=0)
            acc = acc + weight * part.astype(F32)
        result = acc / total
        for g in range(NHEAD):
            cols = slice(g * WIDTH + head * HDIM, g * WIDTH + (head + 1) * HDIM)
            out_first[:, cols] = result[g * 2 * TOK : g * 2 * TOK + TOK].astype(BF16)
            out_second[:, cols] = result[g * 2 * TOK + TOK : (g + 1) * 2 * TOK].astype(BF16)


def vmem(n):
    return [pl.BlockSpec(memory_space=pltpu.VMEM)] * n


def smem(n):
    return [pl.BlockSpec(memory_space=pltpu.SMEM)] * n


PARAMS = pltpu.CompilerParams(vmem_limit_bytes=40 * 1024 * 1024)
PACK_PARAMS = pltpu.CompilerParams(vmem_limit_bytes=62 * 1024 * 1024)


def body(q1, k1, v1, q2, k2, v2, key_stale, value_stale, gate_table, step_index):
    shape = jax.ShapeDtypeStruct
    packed, kv = pl.pallas_call(
        pack_kernel,
        out_shape=(shape((PEERS, BLOCK, WIDTH), BF16), shape((PATCH, 2 * WIDTH), BF16)),
        in_specs=[pl.BlockSpec(memory_space=pltpu.HBM)] * 8,
        out_specs=tuple(vmem(2)),
        scratch_shapes=[pltpu.VMEM((TOK, NHEAD * WIDTH), BF16)] * 6 + [pltpu.SemaphoreType.DMA((8,))],
        compiler_params=PACK_PARAMS,
        name="pack",
    )(q1, k1, v1, q2, k2, v2, key_stale, value_stale)
    recv = lax.all_to_all(packed, PLANE, split_axis=0, concat_axis=0, tiled=True)
    pair = lax.ppermute(kv, "zp", [(0, 1), (1, 0)])
    own = lax.all_gather(jnp.concatenate([kv, pair], axis=0), "zq", axis=0, tiled=True)
    other = lax.ppermute(own, "c", [(0, 1), (1, 0)])
    cost = pl.CostEstimate(flops=4 * ALL * KEYS * WIDTH, bytes_accessed=2 << 20, transcendentals=GROUP * ALL * KEYS)
    state = (shape((ALL, WIDTH), F32),) * 3 + (shape((2 * TOK, WIDTH), F32),)
    state = pl.pallas_call(
        attend_own_kernel,
        out_shape=state,
        in_specs=smem(1) + vmem(3),
        out_specs=tuple(vmem(4)),
        compiler_params=PARAMS,
        cost_estimate=cost,
        name="attend_own",
    )(step_index, recv, own, gate_table)
    partial = pl.pallas_call(
        attend_other_kernel,
        out_shape=shape((2 * SENT * PEERS, HDIM), BF16),
        in_specs=vmem(6),
        out_specs=vmem(1)[0],
        compiler_params=PARAMS,
        cost_estimate=cost,
        name="attend_other",
    )(recv, other, *state)
    back = lax.all_to_all(
        partial.reshape((PEERS, SENT, 2, HDIM)), ("h", "x", "y"), split_axis=0, concat_axis=0, tiled=True
    ).reshape(partial.shape)
    return pl.pallas_call(
        merge_kernel,
        out_shape=(shape((TOK, NHEAD * WIDTH), BF16),) * 2,
        in_specs=vmem(1),
        out_specs=tuple(vmem(2)),
        compiler_params=PARAMS,
        name="merge",
    )(back)


def solution(mesh):
    fine = Mesh(mesh.devices.reshape(NZ // 2, 2, NY, NC, NH, NX), ("zq", "zp", "y", "c", "h", "x"))
    tokens = P(("zq", "zp", "y", "c", "h", "x"), None)
    kept = P(("zq", "zp", "y", "c"), ("h", "x"))
    return jax.shard_map(
        body,
        mesh=fine,
        in_specs=(tokens,) * 6 + (kept, kept, P(None, ("h", "x")), P()),
        out_specs=(tokens, tokens),
        check_vma=False,
    )
```

```python
import functools

import jax
import jax.numpy as jnp
from jax import lax
from jax.experimental import pallas as pl
from jax.experimental.pallas import tpu as pltpu
from jax.sharding import Mesh
from jax.sharding import PartitionSpec as P

HDIM = 128
GROUP = 3
WIDTH = GROUP * HDIM
NZ, NY, NC, NH, NX = 8, 4, 2, 2, 4
NHEAD = NH * NX
PEERS = NY * NHEAD
TOK = 8
PATCH = TOK * NHEAD
FRESH = 2 * TOK // NY
BLOCK = 2 * TOK + 2 * FRESH
SENT = TOK * GROUP + 1
SCALE2 = HDIM ** (-0.5) * 1.4426950408889634
LN2 = 0.6931471805599453
NEG = -1e30
F32 = jnp.float32
BF16 = jnp.bfloat16
PLANE = ("y", "h", "x")


def pack_kernel(q1, k1, v1, q2, k2, v2, ks, vs, out, kv, b0, b1, b2, b3, b4, b5, sems):
    pairs = [(q1, b0), (q2, b1), (k1, b2), (k2, b3), (v1, b4), (v2, b5)]
    pairs += [(ks, kv.at[:, 0:WIDTH]), (vs, kv.at[:, WIDTH : 2 * WIDTH])]
    copies = [pltpu.make_async_copy(src, dst, sems.at[i]) for i, (src, dst) in enumerate(pairs)]
    for copy in copies:
        copy.start()
    share = TOK // NY
    for copy in copies:
        copy.wait()
    for g in range(NHEAD):
        cols = slice(g * WIDTH, (g + 1) * WIDTH)
        queries = jnp.concatenate([b0[:, cols].astype(F32), b1[:, cols].astype(F32)], axis=0).astype(BF16)
        fresh = [ref[:, cols].astype(F32) for ref in (b2, b3, b4, b5)]
        for y in range(NY):
            rows = slice(y * share, (y + 1) * share)
            part = jnp.concatenate([f[rows] for f in fresh], axis=0).astype(BF16)
            out[y * NHEAD + g, 0 : 2 * TOK, :] = queries
            out[y * NHEAD + g, 2 * TOK : BLOCK, :] = part


def split3(x):
    hi = x.astype(BF16)
    rest = x - hi.astype(F32)
    mid = rest.astype(BF16)
    lo = (rest - mid.astype(F32)).astype(BF16)
    return hi, mid, lo


def nt_dot(a, b):
    return lax.dot_general(a, b, (((1,), (1,)), ((), ())), preferred_element_type=F32)


ROWS = 2 * PATCH
ALL = NY * ROWS
FRESH_ROWS = NHEAD * 2 * FRESH
KEYS = NZ * PATCH


def head_cols(head):
    return slice(head * HDIM, (head + 1) * HDIM)


def value_cols(head):
    return slice(WIDTH + head * HDIM, WIDTH + (head + 1) * HDIM)


def queries_of(recv, head):
    return recv[:, 0 : 2 * TOK, head_cols(head)].reshape(ALL, HDIM)


def patch_rows(y):
    return slice(y * ROWS, (y + 1) * ROWS)


def row_max(x):
    return jnp.max(x, axis=1, keepdims=True)


def row_sum(x):
    return jnp.sum(x, axis=1, keepdims=True)


def attend_own_kernel(step_ref, recv, own, gates, acc_out, top_out, total_out, gate_out):
    mine = 2 * lax.axis_index("zq")
    my_y = lax.axis_index("y")
    col = lax.broadcasted_iota(jnp.int32, (1, KEYS), 1)
    own_bias = jnp.where(col // PATCH == mine, NEG, 0.0)
    q_step = (lax.broadcasted_iota(jnp.int32, (ROWS, FRESH_ROWS), 0) // TOK) % 2
    f_kind = lax.broadcasted_iota(jnp.int32, (ROWS, FRESH_ROWS), 1) % (2 * FRESH) // (FRESH // 2)
    fresh_bias = jnp.where(f_kind == q_step, 0.0, NEG)
    at = lax.broadcasted_iota(jnp.int32, (FRESH_ROWS, FRESH_ROWS), 0)
    to = lax.broadcasted_iota(jnp.int32, (FRESH_ROWS, FRESH_ROWS), 1)
    shift = jnp.where(to == at + FRESH, 1.0, 0.0).astype(BF16)
    for step in range(2):
        gate = gates[pl.ds(step_ref[step], 1), :]
        gate_out[step * TOK : (step + 1) * TOK, :] = jnp.broadcast_to(gate, (TOK, WIDTH))

    def scores(head):
        q = queries_of(recv, head)
        extra = []
        for y in range(NY):
            fresh = recv[y * NHEAD : (y + 1) * NHEAD, 2 * TOK : BLOCK, head_cols(head)].astype(F32)
            fresh = fresh.reshape(FRESH_ROWS, HDIM).astype(BF16)
            fresh_v = jnp.dot(shift, fresh, preferred_element_type=F32).astype(BF16)
            extra.append((nt_dot(q[patch_rows(y)], fresh) + fresh_bias, fresh_v))
        return nt_dot(q, own[:, head_cols(head)]), extra

    ready = scores(0)
    for head in range(GROUP):
        s_own, extra = ready
        if head + 1 < GROUP:
            ready = scores(head + 1)
        weights, accs = [], []
        for y in range(NY):
            s_a = s_own[patch_rows(y)] + jnp.where(my_y == y, own_bias, 0.0)
            s_f, fresh_v = extra[y]
            top = jnp.maximum(row_max(s_a), row_max(s_f))
            p_a = jnp.exp2((s_a - top) * SCALE2)
            p_f = jnp.exp2((s_f - top) * SCALE2)
            total = row_sum(p_a) + row_sum(p_f)
            weights.append(p_a.astype(BF16))
            accs.append(jnp.dot(p_f.astype(BF16), fresh_v, preferred_element_type=F32))
            top_out[patch_rows(y), head_cols(head)] = jnp.broadcast_to(top, (ROWS, HDIM))
            total_out[patch_rows(y), head_cols(head)] = jnp.broadcast_to(total, (ROWS, HDIM))
        acc = jnp.dot(jnp.concatenate(weights, axis=0), own[:, value_cols(head)], preferred_element_type=F32)
        acc_out[:, head_cols(head)] = acc + jnp.concatenate(accs, axis=0)


def fold_matrix(height, width, short, long):
    at = lax.broadcasted_iota(jnp.int32, (height, width), short)
    row = lax.broadcasted_iota(jnp.int32, (height, width), long)
    return jnp.where(at == 2 * (row // (2 * TOK)) + row % 2, 1.0, 0.0).astype(BF16)


def attend_other_kernel(recv, other, acc_in, top_in, total_in, gate_in, out):
    lane = lax.broadcasted_iota(jnp.int32, (ROWS, HDIM), 1)
    slot = lane - 3 * GROUP * (lax.broadcasted_iota(jnp.int32, (ROWS, HDIM), 0) // 2 % TOK)
    stats = [jnp.zeros((ROWS, HDIM), F32) for _ in range(NY)]

    def scores(head):
        return nt_dot(queries_of(recv, head), other[:, head_cols(head)])

    ready = scores(0)
    for head in range(GROUP):
        s_all = ready
        if head + 1 < GROUP:
            ready = scores(head + 1)
        weights, tops, totals, keeps = [], [], [], []
        for y in range(NY):
            s_b = s_all[patch_rows(y)]
            old_top = top_in[patch_rows(y), head_cols(head)]
            top = jnp.maximum(jnp.broadcast_to(row_max(s_b), (ROWS, HDIM)), old_top)
            p_b = jnp.exp2((s_b - jnp.concatenate([top] * (KEYS // HDIM), axis=1)) * SCALE2)
            keep = jnp.exp2((old_top - top) * SCALE2)
            tops.append(top)
            keeps.append(keep)
            totals.append(jnp.broadcast_to(row_sum(p_b), (ROWS, HDIM)) + keep * total_in[patch_rows(y), head_cols(head)])
            weights.append(p_b.astype(BF16))
        acc = jnp.dot(jnp.concatenate(weights, axis=0), other[:, value_cols(head)], preferred_element_type=F32)
        cols = head_cols(head)
        gate = jnp.concatenate([gate_in[:, cols]] * NHEAD, axis=0)
        for y in range(NY):
            total = acc[patch_rows(y)] + keeps[y] * acc_in[patch_rows(y), cols]
            mixed = (total / totals[y]) * gate
            out[:, y, head * TOK : (head + 1) * TOK, :, :] = (
                mixed.astype(BF16).reshape(NHEAD, TOK, 2, HDIM)
            )
            size = tops[y] * SCALE2 + jnp.log(totals[y]) * (1.0 / LN2)
            for i, piece in enumerate(split3(size)):
                stats[y] = jnp.where(slot == 3 * head + i, piece.astype(F32), stats[y])
    for y in range(NY):
        for i in range(NHEAD):
            rows = stats[y][2 * TOK * i : 2 * TOK * i + TOK] + stats[y][2 * TOK * i + TOK : 2 * TOK * (i + 1)]
            rows = rows + pltpu.roll(rows, 4, 0)
            rows = rows + pltpu.roll(rows, 2, 0)
            out[i, y, SENT - 1, :, :] = rows[0:2].astype(BF16)


def merge_kernel(recv, out_first, out_second):
    at = lax.broadcasted_iota(jnp.int32, (HDIM, WIDTH), 0)
    to = lax.broadcasted_iota(jnp.int32, (HDIM, WIDTH), 1)
    spread = jnp.where((at % (3 * GROUP)) // 3 == to // HDIM, 1.0, 0.0).astype(BF16)
    lane = lax.broadcasted_iota(jnp.int32, (ALL, HDIM), 1)
    pair = lax.broadcasted_iota(jnp.int32, (ALL, HDIM), 0) // 2 % TOK
    stats = jnp.concatenate([recv[:, y, SENT - 1, :, :].reshape(2 * NHEAD, HDIM) for y in range(NY)], axis=0)
    stats = jnp.dot(fold_matrix(ALL, 2 * PEERS, 1, 0), stats, preferred_element_type=F32)
    stats = jnp.where(lane // (3 * GROUP) == pair, stats, 0.0).astype(BF16)
    sizes = jnp.dot(stats, spread, preferred_element_type=F32)
    for head in range(GROUP):
        size = [sizes[patch_rows(y), head_cols(head)] for y in range(NY)]
        top = functools.reduce(jnp.maximum, size)
        total = jnp.zeros_like(top)
        acc = jnp.zeros_like(top)
        for y in range(NY):
            weight = jnp.exp2(size[y] - top)
            total = total + weight
            part = recv[:, y, head * TOK : (head + 1) * TOK, :, :].reshape(ROWS, HDIM)
            acc = acc + weight * part.astype(F32)
        result = acc / total
        for g in range(NHEAD):
            cols = slice(g * WIDTH + head * HDIM, g * WIDTH + (head + 1) * HDIM)
            out_first[:, cols] = result[g * 2 * TOK : g * 2 * TOK + TOK].astype(BF16)
            out_second[:, cols] = result[g * 2 * TOK + TOK : (g + 1) * 2 * TOK].astype(BF16)


def vmem(n):
    return [pl.BlockSpec(memory_space=pltpu.VMEM)] * n


def smem(n):
    return [pl.BlockSpec(memory_space=pltpu.SMEM)] * n


PARAMS = pltpu.CompilerParams(vmem_limit_bytes=40 * 1024 * 1024)
PACK_PARAMS = pltpu.CompilerParams(vmem_limit_bytes=62 * 1024 * 1024)


def body(q1, k1, v1, q2, k2, v2, key_stale, value_stale, gate_table, step_index):
    shape = jax.ShapeDtypeStruct
    packed, kv = pl.pallas_call(
        pack_kernel,
        out_shape=(shape((PEERS, BLOCK, WIDTH), BF16), shape((PATCH, 2 * WIDTH), BF16)),
        in_specs=[pl.BlockSpec(memory_space=pltpu.HBM)] * 8,
        out_specs=tuple(vmem(2)),
        scratch_shapes=[pltpu.VMEM((TOK, NHEAD * WIDTH), BF16)] * 6 + [pltpu.SemaphoreType.DMA((8,))],
        compiler_params=PACK_PARAMS,
        name="pack",
    )(q1, k1, v1, q2, k2, v2, key_stale, value_stale)
    recv = lax.all_to_all(packed, PLANE, split_axis=0, concat_axis=0, tiled=True)
    pair = lax.ppermute(kv, "zp", [(0, 1), (1, 0)])
    own = lax.all_gather(jnp.concatenate([kv, pair], axis=0), "zq", axis=0, tiled=True)
    other = lax.ppermute(own, "c", [(0, 1), (1, 0)])
    cost = pl.CostEstimate(flops=4 * ALL * KEYS * WIDTH, bytes_accessed=2 << 20, transcendentals=GROUP * ALL * KEYS)
    state = (shape((ALL, WIDTH), F32),) * 3 + (shape((2 * TOK, WIDTH), F32),)
    state = pl.pallas_call(
        attend_own_kernel,
        out_shape=state,
        in_specs=smem(1) + vmem(3),
        out_specs=tuple(vmem(4)),
        compiler_params=PARAMS,
        cost_estimate=cost,
        name="attend_own",
    )(step_index, recv, own, gate_table)
    partial = pl.pallas_call(
        attend_other_kernel,
        out_shape=shape((NHEAD, NY, SENT, 2, HDIM), BF16),
        in_specs=vmem(6),
        out_specs=vmem(1)[0],
        compiler_params=PARAMS,
        cost_estimate=cost,
        name="attend_other",
    )(recv, other, *state)
    back = lax.all_to_all(
        partial.reshape((PEERS,) + partial.shape[2:]), ("h", "x", "y"), split_axis=0, concat_axis=0, tiled=True
    ).reshape(partial.shape)
    return pl.pallas_call(
        merge_kernel,
        out_shape=(shape((TOK, NHEAD * WIDTH), BF16),) * 2,
        in_specs=vmem(1),
        out_specs=tuple(vmem(2)),
        compiler_params=PARAMS,
        name="merge",
    )(back)


def solution(mesh):
    fine = Mesh(mesh.devices.reshape(NZ // 2, 2, NY, NC, NH, NX), ("zq", "zp", "y", "c", "h", "x"))
    tokens = P(("zq", "zp", "y", "c", "h", "x"), None)
    kept = P(("zq", "zp", "y", "c"), ("h", "x"))
    return jax.shard_map(
        body,
        mesh=fine,
        in_specs=(tokens,) * 6 + (kept, kept, P(None, ("h", "x")), P()),
        out_specs=(tokens, tokens),
        check_vma=False,
    )
```

```python
import functools

import jax
import jax.numpy as jnp
from jax import lax
from jax.experimental import pallas as pl
from jax.experimental.pallas import tpu as pltpu
from jax.sharding import Mesh
from jax.sharding import PartitionSpec as P

HDIM = 128
GROUP = 3
WIDTH = GROUP * HDIM
NZ, NY, NC, NH, NX = 8, 4, 2, 2, 4
NHEAD = NH * NX
PEERS = NY * NHEAD
TOK = 8
PATCH = TOK * NHEAD
FRESH = 2 * TOK // NY
BLOCK = 2 * TOK + 2 * FRESH
SENT = TOK * GROUP + 1
SCALE2 = HDIM ** (-0.5) * 1.4426950408889634
LN2 = 0.6931471805599453
NEG = -1e30
F32 = jnp.float32
BF16 = jnp.bfloat16
PLANE = ("h", "x", "y")


def pack_kernel(q1, k1, v1, q2, k2, v2, ks, vs, out, kv, b0, b1, b2, b3, b4, b5, sems):
    pairs = [(q1, b0), (q2, b1), (k1, b2), (k2, b3), (v1, b4), (v2, b5)]
    pairs += [(ks, kv.at[:, 0:WIDTH]), (vs, kv.at[:, WIDTH : 2 * WIDTH])]
    copies = [pltpu.make_async_copy(src, dst, sems.at[i]) for i, (src, dst) in enumerate(pairs)]
    for copy in copies:
        copy.start()
    share = TOK // NY
    for copy in copies:
        copy.wait()
    for g in range(NHEAD):
        cols = slice(g * WIDTH, (g + 1) * WIDTH)
        queries = jnp.concatenate([b0[:, cols].astype(F32), b1[:, cols].astype(F32)], axis=0).astype(BF16)
        fresh = [ref[:, cols].astype(F32) for ref in (b2, b3, b4, b5)]
        for y in range(NY):
            rows = slice(y * share, (y + 1) * share)
            part = jnp.concatenate([f[rows] for f in fresh], axis=0).astype(BF16)
            out[g, y, 0 : 2 * TOK, :] = queries
            out[g, y, 2 * TOK : BLOCK, :] = part


def split3(x):
    hi = x.astype(BF16)
    rest = x - hi.astype(F32)
    mid = rest.astype(BF16)
    lo = (rest - mid.astype(F32)).astype(BF16)
    return hi, mid, lo


def nt_dot(a, b):
    return lax.dot_general(a, b, (((1,), (1,)), ((), ())), preferred_element_type=F32)


ROWS = 2 * PATCH
ALL = NY * ROWS
FRESH_ROWS = NHEAD * 2 * FRESH
KEYS = NZ * PATCH


def head_cols(head):
    return slice(head * HDIM, (head + 1) * HDIM)


def value_cols(head):
    return slice(WIDTH + head * HDIM, WIDTH + (head + 1) * HDIM)


def queries_of(recv, head):
    return jnp.concatenate(
        [recv[:, y, 0 : 2 * TOK, head_cols(head)].reshape(ROWS, HDIM) for y in range(NY)], axis=0
    )


def patch_rows(y):
    return slice(y * ROWS, (y + 1) * ROWS)


def row_max(x):
    return jnp.max(x, axis=1, keepdims=True)


def row_sum(x):
    return jnp.sum(x, axis=1, keepdims=True)


def attend_own_kernel(step_ref, recv, own, gates, acc_out, top_out, total_out, gate_out):
    mine = 2 * lax.axis_index("zq")
    my_y = lax.axis_index("y")
    col = lax.broadcasted_iota(jnp.int32, (1, KEYS), 1)
    own_bias = jnp.where(col // PATCH == mine, NEG, 0.0)
    q_step = (lax.broadcasted_iota(jnp.int32, (ROWS, FRESH_ROWS), 0) // TOK) % 2
    f_kind = lax.broadcasted_iota(jnp.int32, (ROWS, FRESH_ROWS), 1) % (2 * FRESH) // (FRESH // 2)
    fresh_bias = jnp.where(f_kind == q_step, 0.0, NEG)
    at = lax.broadcasted_iota(jnp.int32, (FRESH_ROWS, FRESH_ROWS), 0)
    to = lax.broadcasted_iota(jnp.int32, (FRESH_ROWS, FRESH_ROWS), 1)
    shift = jnp.where(to == at + FRESH, 1.0, 0.0).astype(BF16)
    for step in range(2):
        gate = gates[pl.ds(step_ref[step], 1), :]
        gate_out[step * TOK : (step + 1) * TOK, :] = jnp.broadcast_to(gate, (TOK, WIDTH))

    def scores(head):
        q = queries_of(recv, head)
        extra = []
        for y in range(NY):
            fresh = recv[:, y, 2 * TOK : BLOCK, head_cols(head)].astype(F32)
            fresh = fresh.reshape(FRESH_ROWS, HDIM).astype(BF16)
            fresh_v = jnp.dot(shift, fresh, preferred_element_type=F32).astype(BF16)
            extra.append((nt_dot(q[patch_rows(y)], fresh) + fresh_bias, fresh_v))
        return nt_dot(q, own[:, head_cols(head)]), extra

    ready = scores(0)
    for head in range(GROUP):
        s_own, extra = ready
        if head + 1 < GROUP:
            ready = scores(head + 1)
        weights, accs = [], []
        for y in range(NY):
            s_a = s_own[patch_rows(y)] + jnp.where(my_y == y, own_bias, 0.0)
            s_f, fresh_v = extra[y]
            top = jnp.maximum(row_max(s_a), row_max(s_f))
            p_a = jnp.exp2((s_a - top) * SCALE2)
            p_f = jnp.exp2((s_f - top) * SCALE2)
            total = row_sum(p_a) + row_sum(p_f)
            weights.append(p_a.astype(BF16))
            accs.append(jnp.dot(p_f.astype(BF16), fresh_v, preferred_element_type=F32))
            top_out[patch_rows(y), head_cols(head)] = jnp.broadcast_to(top, (ROWS, HDIM))
            total_out[patch_rows(y), head_cols(head)] = jnp.broadcast_to(total, (ROWS, HDIM))
        acc = jnp.dot(jnp.concatenate(weights, axis=0), own[:, value_cols(head)], preferred_element_type=F32)
        acc_out[:, head_cols(head)] = acc + jnp.concatenate(accs, axis=0)


def fold_matrix(height, width, short, long):
    at = lax.broadcasted_iota(jnp.int32, (height, width), short)
    row = lax.broadcasted_iota(jnp.int32, (height, width), long)
    return jnp.where(at == 2 * (row // (2 * TOK)) + row % 2, 1.0, 0.0).astype(BF16)


def attend_other_kernel(recv, other, acc_in, top_in, total_in, gate_in, out):
    lane = lax.broadcasted_iota(jnp.int32, (ROWS, HDIM), 1)
    slot = lane - 3 * GROUP * (lax.broadcasted_iota(jnp.int32, (ROWS, HDIM), 0) // 2 % TOK)
    stats = [jnp.zeros((ROWS, HDIM), F32) for _ in range(NY)]

    def scores(head):
        return nt_dot(queries_of(recv, head), other[:, head_cols(head)])

    ready = scores(0)
    for head in range(GROUP):
        s_all = ready
        if head + 1 < GROUP:
            ready = scores(head + 1)
        weights, tops, totals, keeps = [], [], [], []
        for y in range(NY):
            s_b = s_all[patch_rows(y)]
            old_top = top_in[patch_rows(y), head_cols(head)]
            top = jnp.maximum(jnp.broadcast_to(row_max(s_b), (ROWS, HDIM)), old_top)
            p_b = jnp.exp2((s_b - jnp.concatenate([top] * (KEYS // HDIM), axis=1)) * SCALE2)
            keep = jnp.exp2((old_top - top) * SCALE2)
            tops.append(top)
            keeps.append(keep)
            totals.append(jnp.broadcast_to(row_sum(p_b), (ROWS, HDIM)) + keep * total_in[patch_rows(y), head_cols(head)])
            weights.append(p_b.astype(BF16))
        acc = jnp.dot(jnp.concatenate(weights, axis=0), other[:, value_cols(head)], preferred_element_type=F32)
        cols = head_cols(head)
        gate = jnp.concatenate([gate_in[:, cols]] * NHEAD, axis=0)
        for y in range(NY):
            total = acc[patch_rows(y)] + keeps[y] * acc_in[patch_rows(y), cols]
            mixed = (total / totals[y]) * gate
            out[:, y, head * TOK : (head + 1) * TOK, :, :] = (
                mixed.astype(BF16).reshape(NHEAD, TOK, 2, HDIM)
            )
            size = tops[y] * SCALE2 + jnp.log(totals[y]) * (1.0 / LN2)
            for i, piece in enumerate(split3(size)):
                stats[y] = jnp.where(slot == 3 * head + i, piece.astype(F32), stats[y])
    for y in range(NY):
        for i in range(NHEAD):
            rows = stats[y][2 * TOK * i : 2 * TOK * i + TOK] + stats[y][2 * TOK * i + TOK : 2 * TOK * (i + 1)]
            rows = rows + pltpu.roll(rows, 4, 0)
            rows = rows + pltpu.roll(rows, 2, 0)
            out[i, y, SENT - 1, :, :] = rows[0:2].astype(BF16)


def merge_kernel(recv, out_first, out_second):
    at = lax.broadcasted_iota(jnp.int32, (HDIM, WIDTH), 0)
    to = lax.broadcasted_iota(jnp.int32, (HDIM, WIDTH), 1)
    spread = jnp.where((at % (3 * GROUP)) // 3 == to // HDIM, 1.0, 0.0).astype(BF16)
    lane = lax.broadcasted_iota(jnp.int32, (ALL, HDIM), 1)
    pair = lax.broadcasted_iota(jnp.int32, (ALL, HDIM), 0) // 2 % TOK
    stats = jnp.concatenate([recv[:, y, SENT - 1, :, :].reshape(2 * NHEAD, HDIM) for y in range(NY)], axis=0)
    stats = jnp.dot(fold_matrix(ALL, 2 * PEERS, 1, 0), stats, preferred_element_type=F32)
    stats = jnp.where(lane // (3 * GROUP) == pair, stats, 0.0).astype(BF16)
    sizes = jnp.dot(stats, spread, preferred_element_type=F32)
    for head in range(GROUP):
        size = [sizes[patch_rows(y), head_cols(head)] for y in range(NY)]
        top = functools.reduce(jnp.maximum, size)
        total = jnp.zeros_like(top)
        acc = jnp.zeros_like(top)
        for y in range(NY):
            weight = jnp.exp2(size[y] - top)
            total = total + weight
            part = recv[:, y, head * TOK : (head + 1) * TOK, :, :].reshape(ROWS, HDIM)
            acc = acc + weight * part.astype(F32)
        result = acc / total
        for g in range(NHEAD):
            cols = slice(g * WIDTH + head * HDIM, g * WIDTH + (head + 1) * HDIM)
            out_first[:, cols] = result[g * 2 * TOK : g * 2 * TOK + TOK].astype(BF16)
            out_second[:, cols] = result[g * 2 * TOK + TOK : (g + 1) * 2 * TOK].astype(BF16)


def vmem(n):
    return [pl.BlockSpec(memory_space=pltpu.VMEM)] * n


def smem(n):
    return [pl.BlockSpec(memory_space=pltpu.SMEM)] * n


PARAMS = pltpu.CompilerParams(vmem_limit_bytes=40 * 1024 * 1024)
PACK_PARAMS = pltpu.CompilerParams(vmem_limit_bytes=62 * 1024 * 1024)


def exchange(blocks):
    flat = blocks.reshape((PEERS,) + blocks.shape[2:])
    return lax.all_to_all(flat, PLANE, split_axis=0, concat_axis=0, tiled=True).reshape(blocks.shape)


def body(q1, k1, v1, q2, k2, v2, key_stale, value_stale, gate_table, step_index):
    shape = jax.ShapeDtypeStruct
    packed, kv = pl.pallas_call(
        pack_kernel,
        out_shape=(shape((NHEAD, NY, BLOCK, WIDTH), BF16), shape((PATCH, 2 * WIDTH), BF16)),
        in_specs=[pl.BlockSpec(memory_space=pltpu.HBM)] * 8,
        out_specs=tuple(vmem(2)),
        scratch_shapes=[pltpu.VMEM((TOK, NHEAD * WIDTH), BF16)] * 6 + [pltpu.SemaphoreType.DMA((8,))],
        compiler_params=PACK_PARAMS,
        name="pack",
    )(q1, k1, v1, q2, k2, v2, key_stale, value_stale)
    recv = exchange(packed)
    pair = lax.ppermute(kv, "zp", [(0, 1), (1, 0)])
    own = lax.all_gather(jnp.concatenate([kv, pair], axis=0), "zq", axis=0, tiled=True)
    other = lax.ppermute(own, "c", [(0, 1), (1, 0)])
    cost = pl.CostEstimate(flops=4 * ALL * KEYS * WIDTH, bytes_accessed=2 << 20, transcendentals=GROUP * ALL * KEYS)
    state = (shape((ALL, WIDTH), F32),) * 3 + (shape((2 * TOK, WIDTH), F32),)
    state = pl.pallas_call(
        attend_own_kernel,
        out_shape=state,
        in_specs=smem(1) + vmem(3),
        out_specs=tuple(vmem(4)),
        compiler_params=PARAMS,
        cost_estimate=cost,
        name="attend_own",
    )(step_index, recv, own, gate_table)
    partial = pl.pallas_call(
        attend_other_kernel,
        out_shape=shape((NHEAD, NY, SENT, 2, HDIM), BF16),
        in_specs=vmem(6),
        out_specs=vmem(1)[0],
        compiler_params=PARAMS,
        cost_estimate=cost,
        name="attend_other",
    )(recv, other, *state)
    back = exchange(partial)
    return pl.pallas_call(
        merge_kernel,
        out_shape=(shape((TOK, NHEAD * WIDTH), BF16),) * 2,
        in_specs=vmem(1),
        out_specs=tuple(vmem(2)),
        compiler_params=PARAMS,
        name="merge",
    )(back)


def solution(mesh):
    fine = Mesh(mesh.devices.reshape(NZ // 2, 2, NY, NC, NH, NX), ("zq", "zp", "y", "c", "h", "x"))
    tokens = P(("zq", "zp", "y", "c", "h", "x"), None)
    kept = P(("zq", "zp", "y", "c"), ("h", "x"))
    return jax.shard_map(
        body,
        mesh=fine,
        in_specs=(tokens,) * 6 + (kept, kept, P(None, ("h", "x")), P()),
        out_specs=(tokens, tokens),
        check_vma=False,
    )
```

```python
import functools

import jax
import jax.numpy as jnp
from jax import lax
from jax.experimental import pallas as pl
from jax.experimental.pallas import tpu as pltpu
from jax.sharding import Mesh
from jax.sharding import PartitionSpec as P

HDIM = 128
GROUP = 3
WIDTH = GROUP * HDIM
NZ, NY, NC, NH, NX = 8, 4, 2, 2, 4
NHEAD = NH * NX
PEERS = NY * NHEAD
TOK = 8
PATCH = TOK * NHEAD
FRESH = 2 * TOK // NY
BLOCK = 2 * TOK + 2 * FRESH
SENT = TOK * GROUP + 1
SCALE2 = HDIM ** (-0.5) * 1.4426950408889634
LN2 = 0.6931471805599453
NEG = -1e30
F32 = jnp.float32
BF16 = jnp.bfloat16
PLANE = ("h", "x", "y")


def pack_kernel(q1, k1, v1, q2, k2, v2, ks, vs, out, kv, b0, b1, b2, b3, b4, b5, sems):
    pairs = [(q1, b0), (q2, b1), (k1, b2), (k2, b3), (v1, b4), (v2, b5)]
    pairs += [(ks, kv.at[:, 0:WIDTH]), (vs, kv.at[:, WIDTH : 2 * WIDTH])]
    copies = [pltpu.make_async_copy(src, dst, sems.at[i]) for i, (src, dst) in enumerate(pairs)]
    for copy in copies:
        copy.start()
    share = TOK // NY
    for copy in copies:
        copy.wait()
    for g in range(NHEAD):
        cols = slice(g * WIDTH, (g + 1) * WIDTH)
        queries = jnp.concatenate([b0[:, cols].astype(F32), b1[:, cols].astype(F32)], axis=0).astype(BF16)
        fresh = [ref[:, cols].astype(F32) for ref in (b2, b3, b4, b5)]
        for y in range(NY):
            rows = slice(y * share, (y + 1) * share)
            part = jnp.concatenate([f[rows] for f in fresh], axis=0).astype(BF16)
            out[g, y, 0 : 2 * TOK, :] = queries
            out[g, y, 2 * TOK : BLOCK, :] = part


def split3(x):
    hi = x.astype(BF16)
    rest = x - hi.astype(F32)
    mid = rest.astype(BF16)
    lo = (rest - mid.astype(F32)).astype(BF16)
    return hi, mid, lo


def nt_dot(a, b):
    return lax.dot_general(a, b, (((1,), (1,)), ((), ())), preferred_element_type=F32)


ROWS = 2 * PATCH
ALL = NY * ROWS
FRESH_ROWS = NHEAD * 2 * FRESH
KEYS = NZ * PATCH


def head_cols(head):
    return slice(head * HDIM, (head + 1) * HDIM)


def value_cols(head):
    return slice(WIDTH + head * HDIM, WIDTH + (head + 1) * HDIM)


def queries_of(recv, head):
    return jnp.concatenate(
        [recv[:, y, 0 : 2 * TOK, head_cols(head)].reshape(ROWS, HDIM) for y in range(NY)], axis=0
    )


def patch_rows(y):
    return slice(y * ROWS, (y + 1) * ROWS)


def row_max(x):
    return jnp.max(x, axis=1, keepdims=True)


def row_sum(x):
    return jnp.sum(x, axis=1, keepdims=True)


def attend_own_kernel(step_ref, recv, own, gates, acc_out, top_out, total_out, gate_out):
    mine = 2 * lax.axis_index("zq")
    my_y = lax.axis_index("y")
    col = lax.broadcasted_iota(jnp.int32, (1, KEYS), 1)
    own_bias = jnp.where(col // PATCH == mine, NEG, 0.0)
    q_step = (lax.broadcasted_iota(jnp.int32, (ROWS, FRESH_ROWS), 0) // TOK) % 2
    f_kind = lax.broadcasted_iota(jnp.int32, (ROWS, FRESH_ROWS), 1) % (2 * FRESH) // (FRESH // 2)
    fresh_bias = jnp.where(f_kind == q_step, 0.0, NEG)
    at = lax.broadcasted_iota(jnp.int32, (FRESH_ROWS, FRESH_ROWS), 0)
    to = lax.broadcasted_iota(jnp.int32, (FRESH_ROWS, FRESH_ROWS), 1)
    shift = jnp.where(to == at + FRESH, 1.0, 0.0).astype(BF16)
    for step in range(2):
        gate = gates[pl.ds(step_ref[step], 1), :]
        gate_out[step * TOK : (step + 1) * TOK, :] = jnp.broadcast_to(gate, (TOK, WIDTH))

    def scores(head):
        q = queries_of(recv, head)
        extra = []
        for y in range(NY):
            fresh = recv[:, y, 2 * TOK : BLOCK, head_cols(head)].astype(F32)
            fresh = fresh.reshape(FRESH_ROWS, HDIM).astype(BF16)
            fresh_v = jnp.dot(shift, fresh, preferred_element_type=F32).astype(BF16)
            extra.append((nt_dot(q[patch_rows(y)], fresh) + fresh_bias, fresh_v))
        return nt_dot(q, own[:, head_cols(head)]), extra

    ready = scores(0)
    for head in range(GROUP):
        s_own, extra = ready
        if head + 1 < GROUP:
            ready = scores(head + 1)
        weights, accs = [], []
        for y in range(NY):
            s_a = s_own[patch_rows(y)] + jnp.where(my_y == y, own_bias, 0.0)
            s_f, fresh_v = extra[y]
            top = jnp.maximum(row_max(s_a), row_max(s_f))
            p_a = jnp.exp2((s_a - top) * SCALE2)
            p_f = jnp.exp2((s_f - top) * SCALE2)
            total = row_sum(p_a) + row_sum(p_f)
            weights.append(p_a.astype(BF16))
            accs.append(jnp.dot(p_f.astype(BF16), fresh_v, preferred_element_type=F32))
            top_out[patch_rows(y), head_cols(head)] = jnp.broadcast_to(top, (ROWS, HDIM))
            total_out[patch_rows(y), head_cols(head)] = jnp.broadcast_to(total, (ROWS, HDIM))
        acc = jnp.dot(jnp.concatenate(weights, axis=0), own[:, value_cols(head)], preferred_element_type=F32)
        acc_out[:, head_cols(head)] = acc + jnp.concatenate(accs, axis=0)


def fold_matrix(height, width, short, long):
    at = lax.broadcasted_iota(jnp.int32, (height, width), short)
    row = lax.broadcasted_iota(jnp.int32, (height, width), long)
    return jnp.where(at == 2 * (row // (2 * TOK)) + row % 2, 1.0, 0.0).astype(BF16)


def attend_other_kernel(recv, other, acc_in, top_in, total_in, gate_in, out):
    lane = lax.broadcasted_iota(jnp.int32, (ROWS, HDIM), 1)
    slot = lane - 3 * GROUP * (lax.broadcasted_iota(jnp.int32, (ROWS, HDIM), 0) // 2 % TOK)
    stats = [jnp.zeros((ROWS, HDIM), F32) for _ in range(NY)]

    def scores(head):
        return nt_dot(queries_of(recv, head), other[:, head_cols(head)])

    ready = scores(0)
    for head in range(GROUP):
        s_all = ready
        if head + 1 < GROUP:
            ready = scores(head + 1)
        weights, tops, totals, keeps = [], [], [], []
        for y in range(NY):
            s_b = s_all[patch_rows(y)]
            old_top = top_in[patch_rows(y), head_cols(head)]
            top = jnp.maximum(jnp.broadcast_to(row_max(s_b), (ROWS, HDIM)), old_top)
            p_b = jnp.exp2((s_b - jnp.concatenate([top] * (KEYS // HDIM), axis=1)) * SCALE2)
            keep = jnp.exp2((old_top - top) * SCALE2)
            tops.append(top)
            keeps.append(keep)
            totals.append(jnp.broadcast_to(row_sum(p_b), (ROWS, HDIM)) + keep * total_in[patch_rows(y), head_cols(head)])
            weights.append(p_b.astype(BF16))
        acc = jnp.dot(jnp.concatenate(weights, axis=0), other[:, value_cols(head)], preferred_element_type=F32)
        cols = head_cols(head)
        gate = jnp.concatenate([gate_in[:, cols]] * NHEAD, axis=0)
        for y in range(NY):
            total = acc[patch_rows(y)] + keeps[y] * acc_in[patch_rows(y), cols]
            mixed = (total / totals[y]) * gate
            mixed = mixed.astype(BF16)
            for i in range(NHEAD):
                start = 2 * SENT * (i * NY + y) + 2 * TOK * head
                out[start : start + 2 * TOK, :] = mixed[2 * TOK * i : 2 * TOK * (i + 1)]
            size = tops[y] * SCALE2 + jnp.log(totals[y]) * (1.0 / LN2)
            for i, piece in enumerate(split3(size)):
                stats[y] = jnp.where(slot == 3 * head + i, piece.astype(F32), stats[y])
    for y in range(NY):
        for i in range(NHEAD):
            rows = stats[y][2 * TOK * i : 2 * TOK * i + TOK] + stats[y][2 * TOK * i + TOK : 2 * TOK * (i + 1)]
            rows = rows + pltpu.roll(rows, 4, 0)
            rows = rows + pltpu.roll(rows, 2, 0)
            start = 2 * SENT * (i * NY + y) + 2 * TOK * GROUP
            out[start : start + 2, :] = rows[0:2].astype(BF16)


def merge_kernel(recv, out_first, out_second):
    at = lax.broadcasted_iota(jnp.int32, (HDIM, WIDTH), 0)
    to = lax.broadcasted_iota(jnp.int32, (HDIM, WIDTH), 1)
    spread = jnp.where((at % (3 * GROUP)) // 3 == to // HDIM, 1.0, 0.0).astype(BF16)
    lane = lax.broadcasted_iota(jnp.int32, (ALL, HDIM), 1)
    pair = lax.broadcasted_iota(jnp.int32, (ALL, HDIM), 0) // 2 % TOK
    stats = jnp.concatenate(
        [recv[pl.ds(2 * SENT * (i * NY + y + 1) - 2, 2), :] for y in range(NY) for i in range(NHEAD)], axis=0
    )
    stats = jnp.dot(fold_matrix(ALL, 2 * PEERS, 1, 0), stats, preferred_element_type=F32)
    stats = jnp.where(lane // (3 * GROUP) == pair, stats, 0.0).astype(BF16)
    sizes = jnp.dot(stats, spread, preferred_element_type=F32)
    for head in range(GROUP):
        size = [sizes[patch_rows(y), head_cols(head)] for y in range(NY)]
        top = functools.reduce(jnp.maximum, size)
        total = jnp.zeros_like(top)
        acc = jnp.zeros_like(top)
        for y in range(NY):
            weight = jnp.exp2(size[y] - top)
            total = total + weight
            starts = [2 * SENT * (i * NY + y) + 2 * TOK * head for i in range(NHEAD)]
            part = jnp.concatenate([recv[a : a + 2 * TOK, :] for a in starts], axis=0)
            acc = acc + weight * part.astype(F32)
        result = acc / total
        for g in range(NHEAD):
            cols = slice(g * WIDTH + head * HDIM, g * WIDTH + (head + 1) * HDIM)
            out_first[:, cols] = result[g * 2 * TOK : g * 2 * TOK + TOK].astype(BF16)
            out_second[:, cols] = result[g * 2 * TOK + TOK : (g + 1) * 2 * TOK].astype(BF16)


def vmem(n):
    return [pl.BlockSpec(memory_space=pltpu.VMEM)] * n


def smem(n):
    return [pl.BlockSpec(memory_space=pltpu.SMEM)] * n


PARAMS = pltpu.CompilerParams(vmem_limit_bytes=40 * 1024 * 1024)
PACK_PARAMS = pltpu.CompilerParams(vmem_limit_bytes=62 * 1024 * 1024)


def exchange(blocks):
    flat = blocks.reshape((PEERS,) + blocks.shape[2:])
    return lax.all_to_all(flat, PLANE, split_axis=0, concat_axis=0, tiled=True).reshape(blocks.shape)


def body(q1, k1, v1, q2, k2, v2, key_stale, value_stale, gate_table, step_index):
    shape = jax.ShapeDtypeStruct
    packed, kv = pl.pallas_call(
        pack_kernel,
        out_shape=(shape((NHEAD, NY, BLOCK, WIDTH), BF16), shape((PATCH, 2 * WIDTH), BF16)),
        in_specs=[pl.BlockSpec(memory_space=pltpu.HBM)] * 8,
        out_specs=tuple(vmem(2)),
        scratch_shapes=[pltpu.VMEM((TOK, NHEAD * WIDTH), BF16)] * 6 + [pltpu.SemaphoreType.DMA((8,))],
        compiler_params=PACK_PARAMS,
        name="pack",
    )(q1, k1, v1, q2, k2, v2, key_stale, value_stale)
    recv = exchange(packed)
    pair = lax.ppermute(kv, "zp", [(0, 1), (1, 0)])
    own = lax.all_gather(jnp.concatenate([kv, pair], axis=0), "zq", axis=0, tiled=True)
    other = lax.ppermute(own, "c", [(0, 1), (1, 0)])
    cost = pl.CostEstimate(flops=4 * ALL * KEYS * WIDTH, bytes_accessed=2 << 20, transcendentals=GROUP * ALL * KEYS)
    state = (shape((ALL, WIDTH), F32),) * 3 + (shape((2 * TOK, WIDTH), F32),)
    state = pl.pallas_call(
        attend_own_kernel,
        out_shape=state,
        in_specs=smem(1) + vmem(3),
        out_specs=tuple(vmem(4)),
        compiler_params=PARAMS,
        cost_estimate=cost,
        name="attend_own",
    )(step_index, recv, own, gate_table)
    partial = pl.pallas_call(
        attend_other_kernel,
        out_shape=shape((2 * SENT * PEERS, HDIM), BF16),
        in_specs=vmem(6),
        out_specs=vmem(1)[0],
        compiler_params=PARAMS,
        cost_estimate=cost,
        name="attend_other",
    )(recv, other, *state)
    back = exchange(partial.reshape((NHEAD, NY, SENT, 2, HDIM))).reshape(partial.shape)
    return pl.pallas_call(
        merge_kernel,
        out_shape=(shape((TOK, NHEAD * WIDTH), BF16),) * 2,
        in_specs=vmem(1),
        out_specs=tuple(vmem(2)),
        compiler_params=PARAMS,
        name="merge",
    )(back)


def solution(mesh):
    fine = Mesh(mesh.devices.reshape(NZ // 2, 2, NY, NC, NH, NX), ("zq", "zp", "y", "c", "h", "x"))
    tokens = P(("zq", "zp", "y", "c", "h", "x"), None)
    kept = P(("zq", "zp", "y", "c"), ("h", "x"))
    return jax.shard_map(
        body,
        mesh=fine,
        in_specs=(tokens,) * 6 + (kept, kept, P(None, ("h", "x")), P()),
        out_specs=(tokens, tokens),
        check_vma=False,
    )
```

```python
import functools

import jax
import jax.numpy as jnp
from jax import lax
from jax.experimental import pallas as pl
from jax.experimental.pallas import tpu as pltpu
from jax.sharding import Mesh
from jax.sharding import PartitionSpec as P

HDIM = 128
GROUP = 3
WIDTH = GROUP * HDIM
NZ, NY, NC, NH, NX = 8, 4, 2, 2, 4
NHEAD = NH * NX
PEERS = NY * NHEAD
TOK = 8
PATCH = TOK * NHEAD
FRESH = 2 * TOK // NY
BLOCK = 2 * TOK + 2 * FRESH
SENT = TOK * GROUP + 1
SCALE2 = HDIM ** (-0.5) * 1.4426950408889634
LN2 = 0.6931471805599453
NEG = -1e30
F32 = jnp.float32
BF16 = jnp.bfloat16
PLANE = ("h", "x", "y")


def pack_kernel(q1, k1, v1, q2, k2, v2, ks, vs, out, kv, b0, b1, b2, b3, b4, b5, sems):
    pairs = [(q1, b0), (q2, b1), (k1, b2), (k2, b3), (v1, b4), (v2, b5)]
    pairs += [(ks, kv.at[:, 0:WIDTH]), (vs, kv.at[:, WIDTH : 2 * WIDTH])]
    copies = [pltpu.make_async_copy(src, dst, sems.at[i]) for i, (src, dst) in enumerate(pairs)]
    for copy in copies:
        copy.start()
    share = TOK // NY
    for copy in copies:
        copy.wait()
    for g in range(NHEAD):
        cols = slice(g * WIDTH, (g + 1) * WIDTH)
        queries = jnp.concatenate([b0[:, cols].astype(F32), b1[:, cols].astype(F32)], axis=0).astype(BF16)
        fresh = [ref[:, cols].astype(F32) for ref in (b2, b3, b4, b5)]
        for y in range(NY):
            rows = slice(y * share, (y + 1) * share)
            part = jnp.concatenate([f[rows] for f in fresh], axis=0).astype(BF16)
            out[g, y, 0 : 2 * TOK, :] = queries
            out[g, y, 2 * TOK : BLOCK, :] = part


def split3(x):
    hi = x.astype(BF16)
    rest = x - hi.astype(F32)
    mid = rest.astype(BF16)
    lo = (rest - mid.astype(F32)).astype(BF16)
    return hi, mid, lo


def nt_dot(a, b):
    return lax.dot_general(a, b, (((1,), (1,)), ((), ())), preferred_element_type=F32)


ROWS = 2 * PATCH
ALL = NY * ROWS
FRESH_ROWS = NHEAD * 2 * FRESH
KEYS = NZ * PATCH


def head_cols(head):
    return slice(head * HDIM, (head + 1) * HDIM)


def value_cols(head):
    return slice(WIDTH + head * HDIM, WIDTH + (head + 1) * HDIM)


def queries_of(recv, head):
    return jnp.concatenate(
        [recv[:, y, 0 : 2 * TOK, head_cols(head)].reshape(ROWS, HDIM) for y in range(NY)], axis=0
    )


def patch_rows(y):
    return slice(y * ROWS, (y + 1) * ROWS)


def row_max(x):
    return jnp.max(x, axis=1, keepdims=True)


def row_sum(x):
    return jnp.sum(x, axis=1, keepdims=True)


def attend_own_kernel(step_ref, recv, own, gates, acc_out, top_out, total_out, gate_out):
    mine = 2 * lax.axis_index("zq")
    my_y = lax.axis_index("y")
    col = lax.broadcasted_iota(jnp.int32, (1, KEYS), 1)
    own_bias = jnp.where(col // PATCH == mine, NEG, 0.0)
    q_step = (lax.broadcasted_iota(jnp.int32, (ROWS, FRESH_ROWS), 0) // TOK) % 2
    f_kind = lax.broadcasted_iota(jnp.int32, (ROWS, FRESH_ROWS), 1) % (2 * FRESH) // (FRESH // 2)
    fresh_bias = jnp.where(f_kind == q_step, 0.0, NEG)
    at = lax.broadcasted_iota(jnp.int32, (FRESH_ROWS, FRESH_ROWS), 0)
    to = lax.broadcasted_iota(jnp.int32, (FRESH_ROWS, FRESH_ROWS), 1)
    shift = jnp.where(to == at + FRESH, 1.0, 0.0).astype(BF16)
    for step in range(2):
        gate = gates[pl.ds(step_ref[step], 1), :]
        gate_out[step * TOK : (step + 1) * TOK, :] = jnp.broadcast_to(gate, (TOK, WIDTH))

    def scores(head):
        q = queries_of(recv, head)
        main = nt_dot(q, own[:, head_cols(head)])
        extra = []
        for y in range(NY):
            fresh = recv[:, y, 2 * TOK : BLOCK, head_cols(head)].astype(F32)
            fresh = fresh.reshape(FRESH_ROWS, HDIM).astype(BF16)
            fresh_v = jnp.dot(shift, fresh, preferred_element_type=F32).astype(BF16)
            extra.append((nt_dot(q[patch_rows(y)], fresh) + fresh_bias, fresh_v))
        return main, extra

    ready = scores(0)
    for head in range(GROUP):
        s_own, extra = ready
        if head + 1 < GROUP:
            ready = scores(head + 1)
        weights, accs = [], []
        for y in range(NY):
            s_a = s_own[patch_rows(y)] + jnp.where(my_y == y, own_bias, 0.0)
            s_f, fresh_v = extra[y]
            top = jnp.maximum(row_max(s_a), row_max(s_f))
            p_a = jnp.exp2((s_a - top) * SCALE2)
            p_f = jnp.exp2((s_f - top) * SCALE2)
            total = row_sum(p_a) + row_sum(p_f)
            weights.append(p_a.astype(BF16))
            accs.append(jnp.dot(p_f.astype(BF16), fresh_v, preferred_element_type=F32))
            top_out[patch_rows(y), head_cols(head)] = jnp.broadcast_to(top, (ROWS, HDIM))
            total_out[patch_rows(y), head_cols(head)] = jnp.broadcast_to(total, (ROWS, HDIM))
        acc = jnp.dot(jnp.concatenate(weights, axis=0), own[:, value_cols(head)], preferred_element_type=F32)
        acc_out[:, head_cols(head)] = acc + jnp.concatenate(accs, axis=0)


def fold_matrix(height, width, short, long):
    at = lax.broadcasted_iota(jnp.int32, (height, width), short)
    row = lax.broadcasted_iota(jnp.int32, (height, width), long)
    return jnp.where(at == 2 * (row // (2 * TOK)) + row % 2, 1.0, 0.0).astype(BF16)


def attend_other_kernel(recv, other, acc_in, top_in, total_in, gate_in, out):
    lane = lax.broadcasted_iota(jnp.int32, (ROWS, HDIM), 1)
    slot = lane - 3 * GROUP * (lax.broadcasted_iota(jnp.int32, (ROWS, HDIM), 0) // 2 % TOK)
    stats = [jnp.zeros((ROWS, HDIM), F32) for _ in range(NY)]

    def scores(head):
        return nt_dot(queries_of(recv, head), other[:, head_cols(head)])

    ready = scores(0)
    for head in range(GROUP):
        s_all = ready
        if head + 1 < GROUP:
            ready = scores(head + 1)
        weights, tops, totals, keeps = [], [], [], []
        for y in range(NY):
            s_b = s_all[patch_rows(y)]
            old_top = top_in[patch_rows(y), head_cols(head)]
            top = jnp.maximum(jnp.broadcast_to(row_max(s_b), (ROWS, HDIM)), old_top)
            p_b = jnp.exp2((s_b - jnp.concatenate([top] * (KEYS // HDIM), axis=1)) * SCALE2)
            keep = jnp.exp2((old_top - top) * SCALE2)
            tops.append(top)
            keeps.append(keep)
            totals.append(jnp.broadcast_to(row_sum(p_b), (ROWS, HDIM)) + keep * total_in[patch_rows(y), head_cols(head)])
            weights.append(p_b.astype(BF16))
        acc = jnp.dot(jnp.concatenate(weights, axis=0), other[:, value_cols(head)], preferred_element_type=F32)
        cols = head_cols(head)
        gate = jnp.concatenate([gate_in[:, cols]] * NHEAD, axis=0)
        for y in range(NY):
            total = acc[patch_rows(y)] + keeps[y] * acc_in[patch_rows(y), cols]
            mixed = (total / totals[y]) * gate
            out[:, y, head * TOK : (head + 1) * TOK, :, :] = (
                mixed.astype(BF16).reshape(NHEAD, TOK, 2, HDIM)
            )
            size = tops[y] * SCALE2 + jnp.log(totals[y]) * (1.0 / LN2)
            for i, piece in enumerate(split3(size)):
                stats[y] = jnp.where(slot == 3 * head + i, piece.astype(F32), stats[y])
    for y in range(NY):
        for i in range(NHEAD):
            rows = stats[y][2 * TOK * i : 2 * TOK * i + TOK] + stats[y][2 * TOK * i + TOK : 2 * TOK * (i + 1)]
            rows = rows + pltpu.roll(rows, 4, 0)
            rows = rows + pltpu.roll(rows, 2, 0)
            out[i, y, SENT - 1, :, :] = rows[0:2].astype(BF16)


def merge_kernel(recv, out_first, out_second):
    at = lax.broadcasted_iota(jnp.int32, (HDIM, WIDTH), 0)
    to = lax.broadcasted_iota(jnp.int32, (HDIM, WIDTH), 1)
    spread = jnp.where((at % (3 * GROUP)) // 3 == to // HDIM, 1.0, 0.0).astype(BF16)
    lane = lax.broadcasted_iota(jnp.int32, (ALL, HDIM), 1)
    pair = lax.broadcasted_iota(jnp.int32, (ALL, HDIM), 0) // 2 % TOK
    stats = jnp.concatenate([recv[:, y, SENT - 1, :, :].reshape(2 * NHEAD, HDIM) for y in range(NY)], axis=0)
    stats = jnp.dot(fold_matrix(ALL, 2 * PEERS, 1, 0), stats, preferred_element_type=F32)
    stats = jnp.where(lane // (3 * GROUP) == pair, stats, 0.0).astype(BF16)
    sizes = jnp.dot(stats, spread, preferred_element_type=F32)
    for head in range(GROUP):
        size = [sizes[patch_rows(y), head_cols(head)] for y in range(NY)]
        top = functools.reduce(jnp.maximum, size)
        total = jnp.zeros_like(top)
        acc = jnp.zeros_like(top)
        for y in range(NY):
            weight = jnp.exp2(size[y] - top)
            total = total + weight
            part = recv[:, y, head * TOK : (head + 1) * TOK, :, :].reshape(ROWS, HDIM)
            acc = acc + weight * part.astype(F32)
        result = acc / total
        for g in range(NHEAD):
            cols = slice(g * WIDTH + head * HDIM, g * WIDTH + (head + 1) * HDIM)
            out_first[:, cols] = result[g * 2 * TOK : g * 2 * TOK + TOK].astype(BF16)
            out_second[:, cols] = result[g * 2 * TOK + TOK : (g + 1) * 2 * TOK].astype(BF16)


def vmem(n):
    return [pl.BlockSpec(memory_space=pltpu.VMEM)] * n


def smem(n):
    return [pl.BlockSpec(memory_space=pltpu.SMEM)] * n


PARAMS = pltpu.CompilerParams(vmem_limit_bytes=40 * 1024 * 1024)
PACK_PARAMS = pltpu.CompilerParams(vmem_limit_bytes=62 * 1024 * 1024)


def exchange(blocks):
    flat = blocks.reshape((PEERS,) + blocks.shape[2:])
    return lax.all_to_all(flat, PLANE, split_axis=0, concat_axis=0, tiled=True).reshape(blocks.shape)


def body(q1, k1, v1, q2, k2, v2, key_stale, value_stale, gate_table, step_index):
    shape = jax.ShapeDtypeStruct
    packed, kv = pl.pallas_call(
        pack_kernel,
        out_shape=(shape((NHEAD, NY, BLOCK, WIDTH), BF16), shape((PATCH, 2 * WIDTH), BF16)),
        in_specs=[pl.BlockSpec(memory_space=pltpu.HBM)] * 8,
        out_specs=tuple(vmem(2)),
        scratch_shapes=[pltpu.VMEM((TOK, NHEAD * WIDTH), BF16)] * 6 + [pltpu.SemaphoreType.DMA((8,))],
        compiler_params=PACK_PARAMS,
        name="pack",
    )(q1, k1, v1, q2, k2, v2, key_stale, value_stale)
    recv = exchange(packed)
    pair = lax.ppermute(kv, "zp", [(0, 1), (1, 0)])
    own = lax.all_gather(jnp.concatenate([kv, pair], axis=0), "zq", axis=0, tiled=True)
    other = lax.ppermute(own, "c", [(0, 1), (1, 0)])
    cost = pl.CostEstimate(flops=4 * ALL * KEYS * WIDTH, bytes_accessed=2 << 20, transcendentals=GROUP * ALL * KEYS)
    state = (shape((ALL, WIDTH), F32),) * 3 + (shape((2 * TOK, WIDTH), F32),)
    state = pl.pallas_call(
        attend_own_kernel,
        out_shape=state,
        in_specs=smem(1) + vmem(3),
        out_specs=tuple(vmem(4)),
        compiler_params=PARAMS,
        cost_estimate=cost,
        name="attend_own",
    )(step_index, recv, own, gate_table)
    partial = pl.pallas_call(
        attend_other_kernel,
        out_shape=shape((NHEAD, NY, SENT, 2, HDIM), BF16),
        in_specs=vmem(6),
        out_specs=vmem(1)[0],
        compiler_params=PARAMS,
        cost_estimate=cost,
        name="attend_other",
    )(recv, other, *state)
    back = exchange(partial)
    return pl.pallas_call(
        merge_kernel,
        out_shape=(shape((TOK, NHEAD * WIDTH), BF16),) * 2,
        in_specs=vmem(1),
        out_specs=tuple(vmem(2)),
        compiler_params=PARAMS,
        name="merge",
    )(back)


def solution(mesh):
    fine = Mesh(mesh.devices.reshape(NZ // 2, 2, NY, NC, NH, NX), ("zq", "zp", "y", "c", "h", "x"))
    tokens = P(("zq", "zp", "y", "c", "h", "x"), None)
    kept = P(("zq", "zp", "y", "c"), ("h", "x"))
    return jax.shard_map(
        body,
        mesh=fine,
        in_specs=(tokens,) * 6 + (kept, kept, P(None, ("h", "x")), P()),
        out_specs=(tokens, tokens),
        check_vma=False,
    )
```
